32 devices in a mesh: dom: 8 (over z, y), grp: 4 (over x, core).
Axes of the slice: x: 2, y: 2, z: 4, core: 2. Of those that a mesh axis runs over, the one named last changes fastest.
Arguments:
- a_strips: bfloat16 [1024, 64, 448], P(('dom', 'grp')), may hold values from -0.25 to 0.25
- p_strips: bfloat16 [1024, 64, 256], P(('dom', 'grp')), may hold values from -1.1953125 to 1.1953125
- nbr_local: int32 [1024, 7], P(('dom', 'grp')), may hold values from 0 to 79, as said below
- ap_slot: int32 [1024, 7, 4], P(('dom', 'grp')), may hold values from 0 to 7, as said below
- tile_slot: int32 [1024, 4, 8], P(('dom', 'grp')), may hold values from 0 to 71, as said below
- send_rows: int32 [32, 8, 6], P(('dom', 'grp')), may hold values from 0 to 31
- owner_map: int32 [32, 72], P(('dom', 'grp')), may hold values from 0 to 127
Outputs:
- coarse_tiles: float32 [64, 262144], P(None, ('dom', 'grp'))
The draws below stay inside these ranges and needn't reach their ends.
Inputs may be any that keep to these rules, and one draw needn't show every extreme that they name: `nbr_local`: column 0 is the element itself. A value below 32 is an element of the same device; the value 32 + p * 6 + g stands for the row that neighbour p sends to this device in slot g, and every such ghost value appears on every device. `ap_slot`: each row's 7 * 4 entries name every value from 0 to 7. `tile_slot`: on every device each of the 72 partial tiles is named by some entry.
All inputs are finite; a program needn't handle non-finite values.
Results may differ from the reference program's by a relative error of at most 0.0029.
Values may be sent and summed in bfloat16 or wider, within the bound.
No kernel may reach another device: no remote copies, remote signals or barrier semaphores. Data moves between devices by JAX's collectives and lax.ppermute only.
A program may use at most 192 MiB of HBM per device.

```python
import math
import jax
import jax.numpy as jnp
from jax import lax

KB = 64
KC = 64
NB = 7
PN = 4
QN = 8
E_DEV = 32
GCAP = 6
SCAP = 8
OWN = 128
NE = 1024
NGHOST = 48
LT = 72
N_DOM = 8
N_GRP = 4


def draw_nbr_local(key, part):
    devices = NE // E_DEV
    positions = E_DEV * (NB - 1)
    row_keys = jax.random.split(jax.random.fold_in(key, 11), devices)

    def per_device(device_key):
        first_key, second_key = jax.random.split(device_key)
        shuffled = jax.random.permutation(first_key, positions)
        local_rows = jax.random.randint(second_key, (positions,), 0, E_DEV)
        picked = jnp.where(shuffled < NGHOST, E_DEV + shuffled, local_rows)
        return picked.reshape(E_DEV, NB - 1)
    others = jax.vmap(per_device)(row_keys).reshape(NE, NB - 1)
    self_col = (jnp.arange(NE) % E_DEV)[:, None]
    return jnp.concatenate([self_col, others], 1).astype(jnp.int32)


def draw_ap_slot(key, part):
    row_keys = jax.random.split(jax.random.fold_in(key, 23), NE)

    def per_row(row_key):
        return (jax.random.permutation(row_key, NB * PN) % QN).reshape(NB, PN)
    return jax.vmap(per_row)(row_keys).astype(jnp.int32)


def draw_tile_slot(key, part):
    devices = NE // E_DEV
    positions = E_DEV * PN * QN
    row_keys = jax.random.split(jax.random.fold_in(key, 37), devices)

    def per_device(device_key):
        first_key, second_key = jax.random.split(device_key)
        shuffled = jax.random.permutation(first_key, positions)
        spread = jax.random.randint(second_key, (positions,), 0, LT)
        picked = jnp.where(shuffled < LT, shuffled, spread)
        return picked.reshape(E_DEV, PN, QN)
    return jax.vmap(per_device)(row_keys).reshape(NE, PN, QN).astype(jnp.int32)


def draw_send_rows(key, part):
    devices = NE // E_DEV
    picked = jax.random.randint(jax.random.fold_in(key, 41), (devices, 8, GCAP), 0, E_DEV)
    picked = picked.at[:, 0, 0].set(E_DEV - 1).at[:, 1, 0].set(0)
    return picked.astype(jnp.int32)


def draw_owner_map(key, part):
    devices = NE // E_DEV
    picked = jax.random.randint(jax.random.fold_in(key, 53), (devices, LT), 0, OWN)
    picked = picked.at[:, 0].set(OWN - 1).at[:, 1].set(0)
    return picked.astype(jnp.int32)


def level_of(rng, shape, pieces, smallest, largest):
    def one(axis_at, parts):
        steps = jax.random.uniform(jax.random.fold_in(jax.random.fold_in(rng, 6), axis_at), (parts,), jnp.float32, smallest / len(pieces), largest / len(pieces))
        return jnp.repeat(jnp.exp(steps), shape[axis_at] // parts).reshape((-1,) + (1,) * (len(shape) - axis_at - 1))

    factor_of = one(*pieces[0])
    for cut in pieces[1:]:
        factor_of = factor_of * one(*cut)
    return factor_of


def scatter_about(stream_key, dims, width, most, cuts=(), kind=jnp.bfloat16):
    values = width * jax.random.normal(stream_key, dims, jnp.float32)
    if cuts:
        values = values * level_of(stream_key, dims, cuts, -0.22, 0.18)
    return jnp.clip(values, -most, most).astype(kind)


def setup_inputs(seed: int = 0) -> dict:
    key_of = jax.random.split(jax.random.key(seed), 8)
    return {
        "a_strips": scatter_about(key_of[0], (NE, KB, NB * KB), (NB * KB) ** -0.5, 0.25, ((0, 32),)),
        "p_strips": scatter_about(key_of[1], (NE, KB, PN * KC), 0.2, 1.1953125, ((0, 32),)),
        "nbr_local": draw_nbr_local(jax.random.fold_in(key_of[7], 71), 0),
        "ap_slot": draw_ap_slot(jax.random.fold_in(key_of[7], 71), 0),
        "tile_slot": draw_tile_slot(jax.random.fold_in(key_of[7], 71), 0),
        "send_rows": draw_send_rows(jax.random.fold_in(key_of[7], 71), 0),
        "owner_map": draw_owner_map(jax.random.fold_in(key_of[7], 71), 0),
    }


def element_terms(a_block, p_block, nbr_block, slot_block, extended):
    block_len = a_block.shape[0]
    a_tiles = a_block.reshape(block_len, KB, NB, KB).astype(jnp.float32)
    gathered = extended[nbr_block].astype(jnp.float32)
    product = jnp.einsum("eijm,ejmn->ejin", a_tiles, gathered, precision=lax.Precision.HIGHEST)
    product = product.reshape(block_len, NB, KB, PN, KC)
    selector = (slot_block[..., None] == jnp.arange(QN, dtype=jnp.int32)).astype(jnp.float32)
    applied = jnp.einsum("ejikc,ejkq->eiqc", product, selector, precision=lax.Precision.HIGHEST)
    applied = lax.optimization_barrier(applied.astype(jnp.bfloat16)).astype(jnp.float32)
    own_tiles = p_block.reshape(block_len, KB, PN, KC).astype(jnp.float32)
    return jnp.einsum("emkc,emqd->ekqcd", own_tiles, applied, precision=lax.Precision.HIGHEST)


def reference(a_strips, p_strips, nbr_local, ap_slot, tile_slot, send_rows, owner_map):
    devices = N_DOM * N_GRP
    tiles_total = 9 * SCAP
    block_len = math.gcd(E_DEV, 32)
    blocks = E_DEV // block_len
    off_rows = jnp.array([-1, -1, -1, 0, 0, 1, 1, 1], dtype=jnp.int32)
    off_cols = jnp.array([-1, 0, 1, -1, 1, -1, 0, 1], dtype=jnp.int32)
    cell_rows = jnp.arange(9, dtype=jnp.int32) // 3 - 1
    cell_cols = jnp.arange(9, dtype=jnp.int32) % 3 - 1

    def per_device(coarse, device):
        dom_at = device // N_GRP
        grp_at = device % N_GRP
        first_row = device * E_DEV
        a_dev = lax.dynamic_slice_in_dim(a_strips, first_row, E_DEV, 0)
        p_dev = lax.dynamic_slice_in_dim(p_strips, first_row, E_DEV, 0)
        nbr_dev = lax.dynamic_slice_in_dim(nbr_local, first_row, E_DEV, 0)
        slot_dev = lax.dynamic_slice_in_dim(ap_slot, first_row, E_DEV, 0)
        tile_dev = lax.dynamic_slice_in_dim(tile_slot, first_row, E_DEV, 0)
        peers = ((dom_at + off_rows) % N_DOM) * N_GRP + (grp_at + off_cols) % N_GRP
        peer_rows = send_rows[peers, 7 - jnp.arange(8, dtype=jnp.int32)]
        sources = (peers[:, None] * E_DEV + peer_rows).reshape(-1)
        extended = jnp.concatenate([p_dev, p_strips[sources]], 0)

        def regroup(source_array):
            return source_array.reshape((blocks, block_len) + source_array.shape[1:])

        def accumulate(partial_value, inputs):
            a_block, p_block, nbr_block, slot_block, tile_block = inputs
            terms = element_terms(a_block, p_block, nbr_block, slot_block, extended)
            partial_value = partial_value.at[tile_block.reshape(-1)].add(terms.reshape(-1, KC, KC))
            return partial_value, None

        initial = jnp.zeros((tiles_total, KC, KC), jnp.float32)
        partial_value = lax.scan(accumulate, initial, (regroup(a_dev), regroup(p_dev), regroup(nbr_dev), regroup(slot_dev), regroup(tile_dev)))[0]
        parcels = partial_value.reshape(9, SCAP, KC, KC)
        owners = ((dom_at + cell_rows) % N_DOM) * N_GRP + (grp_at + cell_cols) % N_GRP
        maps = owner_map[owners].reshape(9, 9, SCAP)
        cells = jnp.arange(9, dtype=jnp.int32)
        targets = maps[cells, 8 - cells]
        coarse = coarse.at[owners[:, None], targets].add(parcels)
        return coarse, None

    coarse = jnp.zeros((devices, OWN, KC, KC), jnp.float32)
    coarse = lax.scan(per_device, coarse, jnp.arange(devices, dtype=jnp.int32))[0]
    return coarse.transpose(2, 0, 1, 3).reshape(KC, devices * OWN * KC)
```

```python
import functools

import jax
import jax.numpy as jnp
from jax import lax
from jax.experimental import pallas as pl
from jax.experimental.pallas import tpu as pltpu
from jax.sharding import PartitionSpec as P

OWN = 128
OFFSETS = ((-1, -1), (-1, 0), (-1, 1), (0, -1), (0, 1), (1, -1), (1, 0), (1, 1))
GROUP = 4
SMEM = pl.BlockSpec(memory_space=pltpu.SMEM)
VMEM = pl.BlockSpec(memory_space=pltpu.VMEM)
ANY = pl.BlockSpec(memory_space=pl.ANY)
LIMIT = 48 * 1024 * 1024


def shifted(x, a, b):
    domains, groups = lax.axis_size("dom"), lax.axis_size("grp")
    pairs = [
        (i * groups + j, ((i + a) % domains) * groups + (j + b) % groups)
        for i in range(domains)
        for j in range(groups)
    ]
    return lax.ppermute(x, ("dom", "grp"), pairs)


def pack_kernel(send_ref, p_ref, *rest):
    outs, sems = rest[:-1], rest[-1]
    copies = [
        pltpu.make_async_copy(p_ref.at[send_ref[0, p, g]], out.at[g], sems.at[p, g])
        for p, out in enumerate(outs)
        for g in range(out.shape[0])
    ]
    for copy in copies:
        copy.start()
    for copy in copies:
        copy.wait()


def pack(send_rows, p_strips):
    _, neighbours, ghosts = send_rows.shape
    return pl.pallas_call(
        pack_kernel,
        out_shape=[jax.ShapeDtypeStruct((ghosts,) + p_strips.shape[1:], p_strips.dtype)] * neighbours,
        in_specs=[SMEM, ANY],
        out_specs=[ANY] * neighbours,
        scratch_shapes=[pltpu.SemaphoreType.DMA((neighbours, ghosts))],
        name="pack",
    )(send_rows, p_strips)


def local_kernel(blocks, pieces, slots, nbr_ref, ap_ref, a_ref, p_ref, sums_ref, ga_ref, pt_ref, info_ref):
    elements, kb, _ = a_ref.shape
    kc = p_ref.shape[2] // pieces
    stride = slots + 1
    left = lax.broadcasted_iota(jnp.int32, (kb, 2 * kc), 1) < kc

    def element(e, count):
        sums_ref[pl.ds(e * stride, stride)] = jnp.zeros((stride, kb, 2 * kc), jnp.float32)
        for j in range(blocks):
            n = nbr_ref[e * blocks + j]
            ghost = n >= elements
            a = a_ref[e, :, j * kb : (j + 1) * kb]
            product = jnp.dot(
                a, p_ref[jnp.where(ghost, 0, n)], preferred_element_type=jnp.float32
            )
            for k in range(pieces):
                slot = ap_ref[(e * blocks + j) * pieces + k]
                row = e * stride + jnp.where(ghost, slots, slot)
                piece = product[:, (k // 2) * 2 * kc : (k // 2 + 1) * 2 * kc]
                sums_ref[row] += jnp.where(left if k % 2 == 0 else ~left, piece, 0.0)
                if j > 0:
                    info_ref[count * (pieces + 1) + k] = e * stride + slot
            if j > 0:
                info_ref[count * (pieces + 1) + pieces] = n - elements
                ga_ref[count] = a
                count = count + ghost.astype(jnp.int32)
        pt = p_ref[e].astype(jnp.float32).T.reshape(pieces, 2, kc // 2, kb)
        pt_ref[e, :, :kb] = pt[:, 0].reshape(pieces * kc // 2, kb).astype(jnp.bfloat16)
        pt_ref[e, :, kb:] = pt[:, 1].reshape(pieces * kc // 2, kb).astype(jnp.bfloat16)
        return count

    count = lax.fori_loop(0, elements, element, jnp.int32(0))
    for u in range(GROUP):
        for k in range(pieces):
            info_ref[(count + u) * (pieces + 1) + k] = slots
        info_ref[(count + u) * (pieces + 1) + pieces] = 0
    info_ref[info_ref.shape[0] - 1] = count


def local_part(a_strips, p_strips, nbr_local, ap_slot, slots):
    elements, kb, _ = a_strips.shape
    blocks, pieces = ap_slot.shape[1:]
    kc = p_strips.shape[2] // pieces
    capacity = elements * (blocks - 1) + GROUP
    return pl.pallas_call(
        functools.partial(local_kernel, blocks, pieces, slots),
        out_shape=[
            pltpu.VMEM((elements * (slots + 1), kb, 2 * kc), jnp.float32),
            pltpu.VMEM((capacity, kb, kb), jnp.bfloat16),
            pltpu.VMEM((elements, pieces * kc // 2, 2 * kb), jnp.bfloat16),
            jax.ShapeDtypeStruct((capacity * (pieces + 1) + 1,), jnp.int32),
        ],
        in_specs=[SMEM, SMEM, VMEM, VMEM],
        out_specs=[VMEM, VMEM, VMEM, SMEM],
        compiler_params=pltpu.CompilerParams(vmem_limit_bytes=LIMIT),
        name="local_part",
    )(nbr_local.reshape(-1), ap_slot.reshape(-1), a_strips, p_strips)


def finish_kernel(pieces, slots, cells, info_ref, tile_ref, sums_ref, ga_ref, pt_ref, *rest):
    arrived = rest[: cells - 1]
    sums_out = rest[cells - 1]
    sent = rest[cells : 2 * cells]
    ghost_ref, tiles_ref, sems = rest[2 * cells :]
    del sums_ref
    ghosts = arrived[0].shape[0]
    elements, _, kb2 = pt_ref.shape
    kb = kb2 // 2
    kc2 = sums_out.shape[2]
    half = kc2 // 4
    stride = slots + 1
    copies = [
        pltpu.make_async_copy(ref, ghost_ref.at[pl.ds(p * ghosts, ghosts)], sems.at[p])
        for p, ref in enumerate(arrived)
    ]
    for copy in copies:
        copy.start()
    tiles_ref[...] = jnp.zeros_like(tiles_ref)
    left = lax.broadcasted_iota(jnp.int32, (kb, kc2), 1) < kc2 // 2
    for copy in copies:
        copy.wait()
    count = info_ref[info_ref.shape[0] - 1]

    def ghost_group(i, carry):
        for u in range(GROUP):
            at = i * GROUP + u
            product = jnp.dot(
                ga_ref[at],
                ghost_ref[info_ref[at * (pieces + 1) + pieces]],
                preferred_element_type=jnp.float32,
            )
            for k in range(pieces):
                piece = product[:, (k // 2) * kc2 : (k // 2 + 1) * kc2]
                sums_out[info_ref[at * (pieces + 1) + k]] += jnp.where(
                    left if k % 2 == 0 else ~left, piece, 0.0
                )
        return carry

    lax.fori_loop(0, (count + GROUP - 1) // GROUP, ghost_group, 0)
    zero = jnp.zeros((kb, kc2), jnp.bfloat16)

    def element(e, carry):
        pt = pt_ref[e]
        for pair in range(slots // 2):
            columns = []
            for q in (2 * pair, 2 * pair + 1):
                x = sums_out[e * stride + q]
                y = (x + pltpu.roll(x, kc2 // 2, 1)).astype(jnp.bfloat16)
                columns.append(
                    jnp.concatenate([jnp.where(left, y, zero), jnp.where(left, zero, y)], axis=0)
                )
            terms = jnp.dot(
                pt, jnp.concatenate(columns, axis=1), preferred_element_type=jnp.float32
            )
            for k in range(pieces):
                for u in range(2):
                    t = tile_ref[(e * pieces + k) * slots + 2 * pair + u]
                    tiles_ref[t] += terms[k * half : (k + 1) * half, u * kc2 : (u + 1) * kc2]
        return carry

    lax.fori_loop(0, elements, element, 0)
    for cell, out in enumerate(sent):
        count_of = out.shape[0]
        out[...] = tiles_ref[pl.ds(cell * count_of, count_of)].astype(out.dtype)


def finish(info, tile_slot, sums, ga, pt, arrived, tiles_total):
    pieces, slots = tile_slot.shape[1:]
    cells = len(arrived) + 1
    half, kc2 = sums.shape[2] // 4, sums.shape[2]
    capacity = tiles_total // cells
    results = pl.pallas_call(
        functools.partial(finish_kernel, pieces, slots, cells),
        out_shape=[pltpu.VMEM(sums.shape, sums.dtype)]
        + [
            jax.ShapeDtypeStruct(
                (capacity, half, kc2), jnp.float32 if cell == cells // 2 else jnp.bfloat16
            )
            for cell in range(cells)
        ],
        in_specs=[SMEM, SMEM, VMEM, VMEM, VMEM] + [ANY] * (cells - 1),
        out_specs=[VMEM] * (cells + 1),
        scratch_shapes=[
            pltpu.VMEM(((cells - 1) * arrived[0].shape[0],) + arrived[0].shape[1:], jnp.bfloat16),
            pltpu.VMEM((tiles_total, half, kc2), jnp.float32),
            pltpu.SemaphoreType.DMA((cells - 1,)),
        ],
        input_output_aliases={2: 0},
        compiler_params=pltpu.CompilerParams(vmem_limit_bytes=LIMIT),
        name="finish",
    )(info, tile_slot.reshape(-1), sums, ga, pt, *arrived)
    return results[1:]


def owner_kernel(owner_ref, *rest):
    parcels, out_ref, tiles_ref = rest[:-2], rest[-2], rest[-1]
    tiles_ref[...] = jnp.zeros_like(tiles_ref)
    owned, half, kc2 = tiles_ref.shape
    for c, parcel in enumerate(parcels):
        capacity = parcel.shape[0]
        for g in range(capacity):
            tiles_ref[owner_ref[c * capacity + g]] += parcel[g].astype(jnp.float32)
    left = lax.broadcasted_iota(jnp.int32, (half, kc2), 1) < kc2 // 2
    for i in range(owned // 2):
        first, second = tiles_ref[2 * i], tiles_ref[2 * i + 1]
        columns = pl.ds(i * kc2, kc2)
        out_ref[:half, columns] = jnp.where(left, first, pltpu.roll(second, kc2 // 2, 1))
        out_ref[half:, columns] = jnp.where(left, pltpu.roll(first, kc2 // 2, 1), second)


def owner_sums(owner_map, parcels):
    _, half, kc2 = parcels[0].shape
    return pl.pallas_call(
        owner_kernel,
        out_shape=jax.ShapeDtypeStruct((2 * half, OWN * kc2 // 2), jnp.float32),
        in_specs=[SMEM] + [VMEM] * len(parcels),
        out_specs=VMEM,
        scratch_shapes=[pltpu.VMEM((OWN, half, kc2), jnp.float32)],
        compiler_params=pltpu.CompilerParams(vmem_limit_bytes=LIMIT),
        name="owner_sums",
    )(owner_map.reshape(-1), *parcels)


def body(a_strips, p_strips, nbr_local, ap_slot, tile_slot, send_rows, owner_map):
    outgoing = pack(send_rows, p_strips)
    arrived = [shifted(outgoing[7 - p], -a, -b) for p, (a, b) in enumerate(OFFSETS)]
    sums, ga, pt, info = local_part(a_strips, p_strips, nbr_local, ap_slot, tile_slot.shape[2])
    tiles = finish(info, tile_slot, sums, ga, pt, arrived, owner_map.shape[1])
    middle = len(tiles) // 2
    returned = [
        tiles[middle]
        if c == middle
        else shifted(tiles[len(tiles) - 1 - c], -(c // 3 - 1), -(c % 3 - 1))
        for c in range(len(tiles))
    ]
    return owner_sums(owner_map, returned)


def solution(mesh):
    placed = (
        P(("dom", "grp"), None, None),
        P(("dom", "grp"), None, None),
        P(("dom", "grp"), None),
        P(("dom", "grp"), None, None),
        P(("dom", "grp"), None, None),
        P(("dom", "grp"), None, None),
        P(("dom", "grp"), None),
    )
    return jax.shard_map(
        body, mesh=mesh, in_specs=placed, out_specs=P(None, ("dom", "grp")), check_vma=False
    )
```

```python
import functools

import jax
import jax.numpy as jnp
from jax import lax
from jax.experimental import pallas as pl
from jax.experimental.pallas import tpu as pltpu
from jax.sharding import PartitionSpec as P

OWN = 128
OFFSETS = ((-1, -1), (-1, 0), (-1, 1), (0, -1), (0, 1), (1, -1), (1, 0), (1, 1))
GROUP = 4
NACC = 4
SMEM = pl.BlockSpec(memory_space=pltpu.SMEM)
VMEM = pl.BlockSpec(memory_space=pltpu.VMEM)
ANY = pl.BlockSpec(memory_space=pl.ANY)
LIMIT = 48 * 1024 * 1024


def resident(x):
    return pltpu.with_memory_space_constraint(x, pltpu.VMEM)


def shifted(x, a, b):
    domains, groups = lax.axis_size("dom"), lax.axis_size("grp")
    pairs = [
        (i * groups + j, ((i + a) % domains) * groups + (j + b) % groups)
        for i in range(domains)
        for j in range(groups)
    ]
    return lax.ppermute(x, ("dom", "grp"), pairs)


def pack_kernel(send_ref, p_ref, *outs):
    for p, out in enumerate(outs):
        for g in range(out.shape[0]):
            out[g] = p_ref[send_ref[0, p, g]]


def pack(send_rows, p_strips):
    _, neighbours, ghosts = send_rows.shape
    return pl.pallas_call(
        pack_kernel,
        out_shape=[pltpu.VMEM((ghosts,) + p_strips.shape[1:], p_strips.dtype)] * neighbours,
        in_specs=[SMEM, VMEM],
        out_specs=[VMEM] * neighbours,
        compiler_params=pltpu.CompilerParams(vmem_limit_bytes=LIMIT),
        name="pack",
    )(send_rows, resident(p_strips))


def local_kernel(blocks, pieces, slots, nbr_ref, ap_ref, a_ref, p_ref, sums_ref, ga_ref, pt_ref, info_ref):
    elements, kb, _ = a_ref.shape
    kc = p_ref.shape[2] // pieces
    stride = slots + 1
    left = lax.broadcasted_iota(jnp.int32, (kb, 2 * kc), 1) < kc

    def element(e, count):
        sums_ref[pl.ds(e * stride, stride)] = jnp.zeros((stride, kb, 2 * kc), jnp.float32)
        for j in range(blocks):
            n = nbr_ref[e * blocks + j]
            ghost = n >= elements
            a = a_ref[e, :, j * kb : (j + 1) * kb]
            product = jnp.dot(
                a, p_ref[jnp.where(ghost, 0, n)], preferred_element_type=jnp.float32
            )
            for k in range(pieces):
                slot = ap_ref[(e * blocks + j) * pieces + k]
                row = e * stride + jnp.where(ghost, slots, slot)
                piece = product[:, (k // 2) * 2 * kc : (k // 2 + 1) * 2 * kc]
                sums_ref[row] += jnp.where(left if k % 2 == 0 else ~left, piece, 0.0)
                if j > 0:
                    info_ref[count * (pieces + 1) + k] = e * stride + slot
            if j > 0:
                info_ref[count * (pieces + 1) + pieces] = n - elements
                ga_ref[count] = a
                count = count + ghost.astype(jnp.int32)
        pt = p_ref[e].astype(jnp.float32).T.reshape(pieces, 2, kc // 2, kb)
        pt_ref[e, :, :kb] = pt[:, 0].reshape(pieces * kc // 2, kb).astype(jnp.bfloat16)
        pt_ref[e, :, kb:] = pt[:, 1].reshape(pieces * kc // 2, kb).astype(jnp.bfloat16)
        return count

    count = lax.fori_loop(0, elements, element, jnp.int32(0))
    for u in range(GROUP):
        for k in range(pieces):
            info_ref[(count + u) * (pieces + 1) + k] = slots
        info_ref[(count + u) * (pieces + 1) + pieces] = 0
    info_ref[info_ref.shape[0] - 1] = count


def local_part(a_strips, p_strips, nbr_local, ap_slot, slots):
    elements, kb, _ = a_strips.shape
    blocks, pieces = ap_slot.shape[1:]
    kc = p_strips.shape[2] // pieces
    capacity = elements * (blocks - 1) + GROUP
    return pl.pallas_call(
        functools.partial(local_kernel, blocks, pieces, slots),
        out_shape=[
            pltpu.VMEM((elements * (slots + 1), kb, 2 * kc), jnp.float32),
            pltpu.VMEM((capacity, kb, kb), jnp.bfloat16),
            pltpu.VMEM((elements, pieces * kc // 2, 2 * kb), jnp.bfloat16),
            jax.ShapeDtypeStruct((capacity * (pieces + 1) + 1,), jnp.int32),
        ],
        in_specs=[SMEM, SMEM, VMEM, VMEM],
        out_specs=[VMEM, VMEM, VMEM, SMEM],
        compiler_params=pltpu.CompilerParams(vmem_limit_bytes=LIMIT),
        name="local_part",
    )(nbr_local.reshape(-1), ap_slot.reshape(-1), a_strips, p_strips)


def finish_kernel(pieces, slots, cells, info_ref, tile_ref, sums_ref, ga_ref, pt_ref, *rest):
    arrived = rest[: cells - 1]
    sums_out = rest[cells - 1]
    sent = rest[cells : 2 * cells]
    ghost_ref, *accs = rest[2 * cells :]
    del sums_ref
    ghosts = arrived[0].shape[0]
    elements, _, kb2 = pt_ref.shape
    kb = kb2 // 2
    kc2 = sums_out.shape[2]
    half = kc2 // 4
    stride = slots + 1
    for p, ref in enumerate(arrived):
        ghost_ref[pl.ds(p * ghosts, ghosts)] = ref[...]
    for acc in accs:
        acc[...] = jnp.zeros_like(acc)
    left = lax.broadcasted_iota(jnp.int32, (kb, kc2), 1) < kc2 // 2
    count = info_ref[info_ref.shape[0] - 1]

    def ghost_group(i, carry):
        for u in range(GROUP):
            at = i * GROUP + u
            product = jnp.dot(
                ga_ref[at],
                ghost_ref[info_ref[at * (pieces + 1) + pieces]],
                preferred_element_type=jnp.float32,
            )
            for k in range(pieces):
                piece = product[:, (k // 2) * kc2 : (k // 2 + 1) * kc2]
                sums_out[info_ref[at * (pieces + 1) + k]] += jnp.where(
                    left if k % 2 == 0 else ~left, piece, 0.0
                )
        return carry

    lax.fori_loop(0, (count + GROUP - 1) // GROUP, ghost_group, 0)
    zero = jnp.zeros((kb, kc2), jnp.bfloat16)

    def one(e):
        pt = pt_ref[e]
        for pair in range(slots // 2):
            columns = []
            for q in (2 * pair, 2 * pair + 1):
                x = sums_out[e * stride + q]
                y = (x + pltpu.roll(x, kc2 // 2, 1)).astype(jnp.bfloat16)
                columns.append(
                    jnp.concatenate([jnp.where(left, y, zero), jnp.where(left, zero, y)], axis=0)
                )
            terms = jnp.dot(
                pt, jnp.concatenate(columns, axis=1), preferred_element_type=jnp.float32
            )
            for k in range(pieces):
                for u in range(2):
                    t = tile_ref[(e * pieces + k) * slots + 2 * pair + u]
                    accs[(k * 2 + u) % len(accs)][t] += terms[k * half : (k + 1) * half, u * kc2 : (u + 1) * kc2]

    def element(i, carry):
        for u in range(4):
            one(i * 4 + u)
        return carry

    lax.fori_loop(0, elements // 4, element, 0)
    for cell, out in enumerate(sent):
        count_of = out.shape[0]
        rows = pl.ds(cell * count_of, count_of)
        out[...] = functools.reduce(jnp.add, [acc[rows] for acc in accs]).astype(out.dtype)


def finish(info, tile_slot, sums, ga, pt, arrived, tiles_total):
    pieces, slots = tile_slot.shape[1:]
    cells = len(arrived) + 1
    half, kc2 = sums.shape[2] // 4, sums.shape[2]
    capacity = tiles_total // cells
    results = pl.pallas_call(
        functools.partial(finish_kernel, pieces, slots, cells),
        out_shape=[pltpu.VMEM(sums.shape, sums.dtype)]
        + [
            pltpu.VMEM((capacity, half, kc2), jnp.float32 if cell == cells // 2 else jnp.bfloat16)
            for cell in range(cells)
        ],
        in_specs=[SMEM, SMEM] + [VMEM] * (cells + 2),
        out_specs=[VMEM] * (cells + 1),
        scratch_shapes=[
            pltpu.VMEM(((cells - 1) * arrived[0].shape[0],) + arrived[0].shape[1:], jnp.bfloat16),
        ]
        + [pltpu.VMEM((tiles_total, half, kc2), jnp.float32)] * NACC,
        input_output_aliases={2: 0},
        compiler_params=pltpu.CompilerParams(vmem_limit_bytes=LIMIT),
        name="finish",
    )(info, tile_slot.reshape(-1), sums, resident(ga), resident(pt), *map(resident, arrived))
    return results[1:]


def owner_kernel(owner_ref, *rest):
    parcels, out_ref, tiles_ref = rest[:-2], rest[-2], rest[-1]
    tiles_ref[...] = jnp.zeros_like(tiles_ref)
    owned, half, kc2 = tiles_ref.shape
    for c, parcel in enumerate(parcels):
        capacity = parcel.shape[0]
        for g in range(capacity):
            tiles_ref[owner_ref[c * capacity + g]] += parcel[g].astype(jnp.float32)
    left = lax.broadcasted_iota(jnp.int32, (half, kc2), 1) < kc2 // 2
    for i in range(owned // 2):
        first, second = tiles_ref[2 * i], tiles_ref[2 * i + 1]
        columns = pl.ds(i * kc2, kc2)
        out_ref[:half, columns] = jnp.where(left, first, pltpu.roll(second, kc2 // 2, 1))
        out_ref[half:, columns] = jnp.where(left, pltpu.roll(first, kc2 // 2, 1), second)


def owner_sums(owner_map, parcels):
    _, half, kc2 = parcels[0].shape
    return pl.pallas_call(
        owner_kernel,
        out_shape=jax.ShapeDtypeStruct((2 * half, OWN * kc2 // 2), jnp.float32),
        in_specs=[SMEM] + [VMEM] * len(parcels),
        out_specs=VMEM,
        scratch_shapes=[pltpu.VMEM((OWN, half, kc2), jnp.float32)],
        compiler_params=pltpu.CompilerParams(vmem_limit_bytes=LIMIT),
        name="owner_sums",
    )(owner_map.reshape(-1), *map(resident, parcels))


def body(a_strips, p_strips, nbr_local, ap_slot, tile_slot, send_rows, owner_map):
    outgoing = pack(send_rows, p_strips)
    arrived = [shifted(outgoing[7 - p], -a, -b) for p, (a, b) in enumerate(OFFSETS)]
    sums, ga, pt, info = local_part(a_strips, p_strips, nbr_local, ap_slot, tile_slot.shape[2])
    tiles = finish(info, tile_slot, sums, ga, pt, arrived, owner_map.shape[1])
    middle = len(tiles) // 2
    returned = [
        tiles[middle]
        if c == middle
        else shifted(tiles[len(tiles) - 1 - c], -(c // 3 - 1), -(c % 3 - 1))
        for c in range(len(tiles))
    ]
    return owner_sums(owner_map, returned)


def solution(mesh):
    placed = (
        P(("dom", "grp"), None, None),
        P(("dom", "grp"), None, None),
        P(("dom", "grp"), None),
        P(("dom", "grp"), None, None),
        P(("dom", "grp"), None, None),
        P(("dom", "grp"), None, None),
        P(("dom", "grp"), None),
    )
    return jax.shard_map(
        body, mesh=mesh, in_specs=placed, out_specs=P(None, ("dom", "grp")), check_vma=False
    )
```

```python
import functools

import jax
import jax.numpy as jnp
from jax import lax
from jax.experimental import pallas as pl
from jax.experimental.pallas import tpu as pltpu
from jax.sharding import PartitionSpec as P

OWN = 128
GROUP = 4
STEP = 4
SUMS = 4
SMEM = pl.BlockSpec(memory_space=pltpu.SMEM)
VMEM = pl.BlockSpec(memory_space=pltpu.VMEM)
ANY = pl.BlockSpec(memory_space=pl.ANY)
PARAMS = pltpu.CompilerParams(vmem_limit_bytes=12 * 1024 * 1024)


def moved(x, a, along):
    domains, groups = lax.axis_size("dom"), lax.axis_size("grp")

    def target(j):
        if along == "pair":
            return j ^ 1
        if along == "far":
            return (j - 1 + 2 * (j % 2)) % groups
        return j

    pairs = [
        (i * groups + j, (i + a) % domains * groups + target(j))
        for i in range(domains)
        for j in range(groups)
    ]
    return lax.ppermute(x, ("dom", "grp"), pairs)


def resident(x):
    return pltpu.with_memory_space_constraint(x, pltpu.VMEM)


def exchange(parts):
    pair, up_far, down_far, far, up, down = parts
    size = up.shape[0]
    pair = moved(pair, 0, "pair")
    up = moved(jnp.concatenate([up, pair[size : 2 * size]]), 1, "own")
    down = moved(jnp.concatenate([down, pair[2 * size :]]), -1, "own")
    return pair, moved(up_far, 1, "far"), moved(down_far, -1, "far"), moved(far, 0, "far"), up, down


def pair_offset():
    return 1 - 2 * (lax.axis_index("grp") % 2)


def sent_cells(offset):
    return (
        (4 + offset, 7 + offset, 1 + offset),
        (7 - offset,),
        (1 - offset,),
        (4 - offset,),
        (7,),
        (1,),
    )


def arrived_cells(offset):
    return ((4 + offset,), (1 - offset,), (7 - offset,), (4 - offset,), (1, 1 + offset), (7, 7 + offset))


EARLY, LATE = (0, 1, 2, 3), (4, 5)


def neighbour_of(cell):
    return cell - jnp.where(cell > 4, 1, 0)


def pack_kernel(send_ref, p_ref, *rest):
    outs, sems = rest[:-1], rest[-1]
    ghosts = send_ref.shape[0]
    copies = []
    for out, cells in zip(outs, sent_cells(pair_offset())):
        for at, cell in enumerate(cells):
            p = neighbour_of(cell)
            for g in range(ghosts):
                copies.append(
                    pltpu.make_async_copy(
                        p_ref.at[send_ref[g, 0, p]], out.at[at * ghosts + g], sems.at[len(copies)]
                    )
                )
    for copy in copies:
        copy.start()
    for copy in copies:
        copy.wait()


def pack(send_rows, p_strips):
    ghosts = send_rows.shape[2]
    return pl.pallas_call(
        pack_kernel,
        out_shape=[
            pltpu.VMEM((len(cells) * ghosts,) + p_strips.shape[1:], p_strips.dtype)
            for cells in sent_cells(1)
        ],
        in_specs=[SMEM, ANY],
        out_specs=[VMEM] * 6,
        scratch_shapes=[pltpu.SemaphoreType.DMA((8 * ghosts,))],
        compiler_params=PARAMS,
        name="pack",
    )(send_rows.transpose(2, 0, 1), p_strips)


def local_kernel(ghosts, slots, nbr_ref, ap_ref, a_ref, p_ref, *rest):
    even_ref, odd_ref, ga_ref, pt_ref, info_ref, order_ref, late_ref = rest
    blocks, pieces, elements = ap_ref.shape
    kb = a_ref.shape[1]
    kc = p_ref.shape[2] // pieces
    stride = slots + 1
    capacity = ga_ref.shape[0] // 2
    offset = pair_offset()
    for cell in (0, 1, 2, 3, 5, 6, 7, 8):
        late = jnp.int32(cell // 3 != 1)
        if cell % 3 != 1:
            late = late * (cell % 3 - 1 == offset).astype(jnp.int32)
        for g in range(ghosts):
            late_ref[(cell - (cell > 4)) * ghosts + g] = late

    def element(e, carry):
        early_count, late_count, early_elements, late_elements = carry
        for ref in (even_ref, odd_ref):
            ref[pl.ds(e * stride, stride)] = jnp.zeros((stride,) + ref.shape[1:], jnp.float32)
        waits = jnp.int32(0)
        for j in range(blocks):
            n = nbr_ref[j, e]
            ghost = n >= elements
            a = a_ref[e, :, j * kb : (j + 1) * kb]
            product = jnp.dot(
                a, p_ref[jnp.where(ghost, 0, n)], preferred_element_type=jnp.float32
            )
            for k in range(pieces):
                row = e * stride + jnp.where(ghost, slots, ap_ref[j, k, e])
                piece = product[:, (k // 2) * 2 * kc : (k // 2 + 1) * 2 * kc]
                ref = odd_ref if k % 2 else even_ref
                ref[row] += piece
            if j > 0:
                late = late_ref[jnp.where(ghost, n - elements, 0)]
                at = jnp.where(late == 1, capacity + late_count, early_count)
                for k in range(pieces):
                    info_ref[at * (pieces + 1) + k] = e * stride + ap_ref[j, k, e]
                info_ref[at * (pieces + 1) + pieces] = n - elements
                ga_ref[at] = a
                is_ghost = ghost.astype(jnp.int32)
                late_count += is_ghost * late
                early_count += is_ghost * (1 - late)
                waits = jnp.maximum(waits, is_ghost * late)
        order_ref[jnp.where(waits == 1, elements - 1 - late_elements, early_elements)] = e
        pt = p_ref[e].astype(jnp.float32).T.reshape(pieces, 2, kc // 2, kb)
        pt_ref[e, :, :kb] = pt[:, 0].reshape(pieces * kc // 2, kb).astype(jnp.bfloat16)
        pt_ref[e, :, kb:] = pt[:, 1].reshape(pieces * kc // 2, kb).astype(jnp.bfloat16)
        return early_count, late_count, early_elements + 1 - waits, late_elements + waits

    zero = jnp.int32(0)
    early_count, late_count, early_elements, _ = lax.fori_loop(
        0, elements, element, (zero, zero, zero, zero)
    )
    for start in (early_count, capacity + late_count):
        for u in range(GROUP):
            for k in range(pieces):
                info_ref[(start + u) * (pieces + 1) + k] = slots
            info_ref[(start + u) * (pieces + 1) + pieces] = 0
    order_ref[elements] = early_elements // STEP
    order_ref[elements + 1] = (early_count + GROUP - 1) // GROUP
    order_ref[elements + 2] = (late_count + GROUP - 1) // GROUP


def local_part(a_strips, p_strips, nbr_local, ap_slot, slots, ghosts):
    elements, kb, _ = a_strips.shape
    blocks, pieces = ap_slot.shape[1:]
    kc = p_strips.shape[2] // pieces
    capacity = elements * (blocks - 1) + GROUP
    sums = pltpu.VMEM((elements * (slots + 1), kb, 2 * kc), jnp.float32)
    return pl.pallas_call(
        functools.partial(local_kernel, ghosts, slots),
        out_shape=[
            sums,
            sums,
            pltpu.VMEM((2 * capacity, kb, kb), jnp.bfloat16),
            pltpu.VMEM((elements, pieces * kc // 2, 2 * kb), jnp.bfloat16),
            jax.ShapeDtypeStruct((2 * capacity * (pieces + 1),), jnp.int32),
            jax.ShapeDtypeStruct((elements + 3,), jnp.int32),
        ],
        in_specs=[SMEM, SMEM, VMEM, VMEM],
        out_specs=[VMEM] * 4 + [SMEM] * 2,
        scratch_shapes=[pltpu.SMEM((8 * ghosts,), jnp.int32)],
        compiler_params=PARAMS,
        cost_estimate=pl.CostEstimate(flops=5 * 10**9, bytes_accessed=10**7, transcendentals=0),
        name="local_part",
    )(nbr_local.T, ap_slot.transpose(1, 2, 0), a_strips, p_strips)


def finish_kernel(late, info_ref, order_ref, tile_ref, ga_ref, pt_ref, *rest):
    parts = LATE if late else EARLY
    arrived, rest = rest[: len(parts)], rest[len(parts) :]
    rest = rest[2 + SUMS * late :]
    even_ref, odd_ref, *tiles = rest[: 2 + SUMS]
    sent, ghost_ref = rest[2 + SUMS : -1], rest[-1]
    pieces, slots, elements = tile_ref.shape
    kb, kc2 = even_ref.shape[1:]
    half = kc2 // 4
    stride = slots + 1
    ghosts = ghost_ref.shape[0] // 8
    first = ga_ref.shape[0] // 2 if late else 0
    offset = pair_offset()
    for part, ref in zip(parts, arrived):
        for at, cell in enumerate(arrived_cells(offset)[part]):
            rows = pl.ds(neighbour_of(cell) * ghosts, ghosts)
            ghost_ref[rows] = ref[at * ghosts : (at + 1) * ghosts]
    if not late:
        for ref in tiles:
            ref[...] = jnp.zeros_like(ref)
    left = lax.broadcasted_iota(jnp.int32, (kb, kc2), 1) < kc2 // 2

    def ghost_group(i, carry):
        for u in range(GROUP):
            at = first + i * GROUP + u
            product = jnp.dot(
                ga_ref[at],
                ghost_ref[info_ref[at * (pieces + 1) + pieces]],
                preferred_element_type=jnp.float32,
            )
            for k in range(pieces):
                ref = odd_ref if k % 2 else even_ref
                ref[info_ref[at * (pieces + 1) + k]] += product[
                    :, (k // 2) * kc2 : (k // 2 + 1) * kc2
                ]
        return carry

    lax.fori_loop(0, order_ref[elements + 1 + late], ghost_group, 0)
    zero = jnp.zeros((kb, kc2), jnp.bfloat16)

    def one(e):
        pt = pt_ref[e]
        for pair in range(slots // 2):
            columns = []
            for q in (2 * pair, 2 * pair + 1):
                x = jnp.where(left, even_ref[e * stride + q], odd_ref[e * stride + q])
                y = (x + pltpu.roll(x, kc2 // 2, 1)).astype(jnp.bfloat16)
                columns.append(
                    jnp.concatenate([jnp.where(left, y, zero), jnp.where(left, zero, y)], axis=0)
                )
            terms = jnp.dot(
                pt, jnp.concatenate(columns, axis=1), preferred_element_type=jnp.float32
            )
            for k in range(pieces):
                for u in range(2):
                    ref = tiles[(2 * k + u) % SUMS]
                    ref[tile_ref[k, 2 * pair + u, e]] += terms[
                        k * half : (k + 1) * half, u * kc2 : (u + 1) * kc2
                    ]

    def step(i, carry):
        for u in range(STEP):
            one(order_ref[i * STEP + u])
        return carry

    early_steps = order_ref[elements]
    if not late:
        lax.fori_loop(0, early_steps, step, 0)
        return
    lax.fori_loop(early_steps, elements // STEP, step, 0)
    capacity = sent[-1].shape[0]

    def total(cell):
        rows = pl.ds(cell * capacity, capacity)
        return functools.reduce(jnp.add, [ref[rows] for ref in tiles])

    for out, cells in zip(sent, sent_cells(offset)):
        for at, cell in enumerate(cells):
            out[at * capacity : (at + 1) * capacity] = total(cell).astype(out.dtype)
    sent[-1][...] = total(4)


def finish(late, info, order, tile_slot, ga, pt, arrived, sums, tiles_total):
    parts = LATE if late else EARLY
    kb, kc2 = sums[0].shape[1:]
    half = kc2 // 4
    capacity = tiles_total // 9
    out_shape = [pltpu.VMEM(x.shape, x.dtype) for x in sums[:2]]
    out_shape += [pltpu.VMEM((tiles_total, half, kc2), jnp.float32)] * SUMS
    if late:
        out_shape += [
            pltpu.VMEM((len(cells) * capacity, half, kc2), jnp.bfloat16) for cells in sent_cells(1)
        ]
        out_shape += [pltpu.VMEM((capacity, half, kc2), jnp.float32)]
    ghost = arrived[0].shape[1:]
    inputs = 5 + len(parts)
    return pl.pallas_call(
        functools.partial(finish_kernel, late),
        out_shape=out_shape,
        in_specs=[SMEM] * 3 + [VMEM] * (2 + len(parts) + len(sums)),
        out_specs=[VMEM] * len(out_shape),
        scratch_shapes=[pltpu.VMEM((8 * (arrived[3].shape[0]),) + ghost, jnp.bfloat16)],
        input_output_aliases={inputs + i: i for i in range(len(sums))},
        compiler_params=PARAMS,
        cost_estimate=pl.CostEstimate(flops=2 * 10**9, bytes_accessed=10**6, transcendentals=0),
        name="late_part" if late else "early_part",
    )(
        info,
        order,
        tile_slot.transpose(1, 2, 0),
        resident(ga),
        resident(pt),
        *(resident(arrived[part]) for part in parts),
        *sums,
    )


def owner_kernel(owner_ref, *rest):
    own, parcels, out_ref, tiles_ref = rest[0], rest[1:-2], rest[-2], rest[-1]
    tiles_ref[...] = jnp.zeros_like(tiles_ref)
    owned, half, kc2 = tiles_ref.shape
    capacity = own.shape[0]

    def add(cell, parcel, at):
        for g in range(capacity):
            tiles_ref[owner_ref[0, cell * capacity + g]] += parcel[at * capacity + g].astype(
                jnp.float32
            )

    add(4, own, 0)
    for parcel, cells in zip(parcels, arrived_cells(pair_offset())):
        for at, cell in enumerate(cells):
            add(cell, parcel, at)
    left = lax.broadcasted_iota(jnp.int32, (half, kc2), 1) < kc2 // 2
    for i in range(owned // 2):
        first, second = tiles_ref[2 * i], tiles_ref[2 * i + 1]
        columns = pl.ds(i * kc2, kc2)
        out_ref[:half, columns] = jnp.where(left, first, pltpu.roll(second, kc2 // 2, 1))
        out_ref[half:, columns] = jnp.where(left, pltpu.roll(first, kc2 // 2, 1), second)


def owner_sums(owner_map, own, parcels):
    _, half, kc2 = own.shape
    return pl.pallas_call(
        owner_kernel,
        out_shape=jax.ShapeDtypeStruct((2 * half, OWN * kc2 // 2), jnp.float32),
        in_specs=[SMEM] + [VMEM] * 7,
        out_specs=VMEM,
        scratch_shapes=[pltpu.VMEM((OWN, half, kc2), jnp.float32)],
        compiler_params=PARAMS,
        name="owner_sums",
    )(owner_map, resident(own), *map(resident, parcels))


def body(a_strips, p_strips, nbr_local, ap_slot, tile_slot, send_rows, owner_map):
    tiles_total = owner_map.shape[1]
    arrived = exchange(pack(send_rows, p_strips))
    *sums, ga, pt, info, order = local_part(
        a_strips, p_strips, nbr_local, ap_slot, tile_slot.shape[2], send_rows.shape[2]
    )
    sums = finish(False, info, order, tile_slot, ga, pt, arrived, sums, tiles_total)
    results = finish(True, info, order, tile_slot, ga, pt, arrived, sums, tiles_total)
    *parcels, own = results[2 + SUMS :]
    return owner_sums(owner_map, own, exchange(parcels))


def solution(mesh):
    placed = (
        P(("dom", "grp"), None, None),
        P(("dom", "grp"), None, None),
        P(("dom", "grp"), None),
        P(("dom", "grp"), None, None),
        P(("dom", "grp"), None, None),
        P(("dom", "grp"), None, None),
        P(("dom", "grp"), None),
    )
    return jax.shard_map(
        body, mesh=mesh, in_specs=placed, out_specs=P(None, ("dom", "grp")), check_vma=False
    )
```

```python
import functools

import jax
import jax.numpy as jnp
from jax import lax
from jax.experimental import pallas as pl
from jax.experimental.pallas import tpu as pltpu
from jax.sharding import PartitionSpec as P

OWN = 128
GROUP = 4
STEP = 4
SUMS = 4
SMEM = pl.BlockSpec(memory_space=pltpu.SMEM)
VMEM = pl.BlockSpec(memory_space=pltpu.VMEM)
HBM = pl.BlockSpec(memory_space=pltpu.HBM)
PARAMS = pltpu.CompilerParams(vmem_limit_bytes=12 * 1024 * 1024)


def moved(x, a, along):
    domains, groups = lax.axis_size("dom"), lax.axis_size("grp")

    def target(j):
        if along == "pair":
            return j ^ 1
        if along == "far":
            return (j - 1 + 2 * (j % 2)) % groups
        return j

    pairs = [
        (i * groups + j, (i + a) % domains * groups + target(j))
        for i in range(domains)
        for j in range(groups)
    ]
    return lax.ppermute(x, ("dom", "grp"), pairs)


def resident(x):
    return pltpu.with_memory_space_constraint(x, pltpu.VMEM)


def exchange(parts, started=None, beside=None):
    pair, far, up, down = parts
    size = up.shape[0]
    pair, far = moved(pair, 0, "pair"), moved(far, 0, "far")
    up, down = jnp.concatenate([up, pair[size : 2 * size]]), jnp.concatenate([down, pair[2 * size :]])
    if beside is not None:
        up, down, started = lax.optimization_barrier((up, down, started))
        result, done = beside(started)
        far, done = lax.optimization_barrier((far, done))
        result = *result, done
    else:
        result = None
    up, down = moved(up, 1, "own"), moved(down, -1, "own")
    up_far = moved(far[size : 2 * size], 1, "own")
    down_far = moved(far[2 * size :], -1, "own")
    return result, (pair, far, up, down, up_far, down_far)


def pair_offset():
    return 1 - 2 * (lax.axis_index("grp") % 2)


def sent_cells(offset):
    return (4 + offset, 7 + offset, 1 + offset), (4 - offset, 7 - offset, 1 - offset), (7,), (1,)


def arrived_cells(offset):
    return (4 + offset,), (4 - offset,), (1, 1 + offset), (7, 7 + offset), (1 - offset,), (7 - offset,)


EARLY, LATE = (0, 1, 2, 3), (4, 5)


def neighbour_of(cell):
    return cell - jnp.where(cell > 4, 1, 0)


def pack_kernel(send_hbm, p_hbm, *rest):
    outs, (send_ref, p_ref, sems) = rest[:-3], rest[-3:]
    ghosts = send_ref.shape[0]
    copies = [
        pltpu.make_async_copy(send_hbm, send_ref, sems.at[0]),
        pltpu.make_async_copy(p_hbm, p_ref, sems.at[1]),
    ]
    for copy in copies:
        copy.start()
    for copy in copies:
        copy.wait()
    for out, cells in zip(outs, sent_cells(pair_offset())):
        for at, cell in enumerate(cells):
            p = neighbour_of(cell)
            for g in range(ghosts):
                out[at * ghosts + g] = p_ref[send_ref[g, 0, p]]


def pack(send_rows, p_strips):
    ghosts = send_rows.shape[2]
    send = send_rows.transpose(2, 0, 1)
    return pl.pallas_call(
        pack_kernel,
        out_shape=[
            pltpu.VMEM((len(cells) * ghosts,) + p_strips.shape[1:], p_strips.dtype)
            for cells in sent_cells(1)
        ],
        in_specs=[HBM, HBM],
        out_specs=[VMEM] * 4,
        scratch_shapes=[
            pltpu.SMEM(send.shape, jnp.int32),
            pltpu.VMEM(p_strips.shape, p_strips.dtype),
            pltpu.SemaphoreType.DMA((2,)),
        ],
        compiler_params=PARAMS,
        name="pack",
    )(
        pltpu.with_memory_space_constraint(send, pltpu.HBM),
        pltpu.with_memory_space_constraint(p_strips, pltpu.HBM),
    )


def local_kernel(ghosts, slots, nbr_ref, ap_ref, a_ref, p_ref, *rest):
    even_ref, odd_ref, ga_ref, pt_ref, info_ref, order_ref, late_ref = rest
    blocks, pieces, elements = ap_ref.shape
    kb = a_ref.shape[1]
    kc = p_ref.shape[2] // pieces
    stride = slots + 1
    capacity = ga_ref.shape[0] // 2
    offset = pair_offset()
    for cell in (0, 1, 2, 3, 5, 6, 7, 8):
        late = jnp.int32(0)
        if cell // 3 != 1 and cell % 3 != 1:
            late = (cell % 3 - 1 == -offset).astype(jnp.int32)
        for g in range(ghosts):
            late_ref[(cell - (cell > 4)) * ghosts + g] = late

    def element(e, carry):
        early_count, late_count, early_elements, late_elements = carry
        for ref in (even_ref, odd_ref):
            ref[pl.ds(e * stride, stride)] = jnp.zeros((stride,) + ref.shape[1:], jnp.float32)
        waits = jnp.int32(0)
        for j in range(blocks):
            n = nbr_ref[j, e]
            ghost = n >= elements
            a = a_ref[e, :, j * kb : (j + 1) * kb]
            product = jnp.dot(
                a, p_ref[jnp.where(ghost, 0, n)], preferred_element_type=jnp.float32
            )
            for k in range(pieces):
                row = e * stride + jnp.where(ghost, slots, ap_ref[j, k, e])
                piece = product[:, (k // 2) * 2 * kc : (k // 2 + 1) * 2 * kc]
                ref = odd_ref if k % 2 else even_ref
                ref[row] += piece
            if j > 0:
                late = late_ref[jnp.where(ghost, n - elements, 0)]
                at = jnp.where(late == 1, capacity + late_count, early_count)
                for k in range(pieces):
                    info_ref[at * (pieces + 1) + k] = e * stride + ap_ref[j, k, e]
                info_ref[at * (pieces + 1) + pieces] = n - elements
                ga_ref[at] = a
                is_ghost = ghost.astype(jnp.int32)
                late_count += is_ghost * late
                early_count += is_ghost * (1 - late)
                waits = jnp.maximum(waits, is_ghost * late)
        order_ref[jnp.where(waits == 1, elements - 1 - late_elements, early_elements)] = e
        pt = p_ref[e].astype(jnp.float32).T.reshape(pieces, 2, kc // 2, kb)
        pt_ref[e, :, :kb] = pt[:, 0].reshape(pieces * kc // 2, kb).astype(jnp.bfloat16)
        pt_ref[e, :, kb:] = pt[:, 1].reshape(pieces * kc // 2, kb).astype(jnp.bfloat16)
        return early_count, late_count, early_elements + 1 - waits, late_elements + waits

    zero = jnp.int32(0)
    early_count, late_count, early_elements, _ = lax.fori_loop(
        0, elements, element, (zero, zero, zero, zero)
    )
    for start in (early_count, capacity + late_count):
        for u in range(GROUP):
            for k in range(pieces):
                info_ref[(start + u) * (pieces + 1) + k] = slots
            info_ref[(start + u) * (pieces + 1) + pieces] = 0
    order_ref[elements] = early_elements // STEP
    order_ref[elements + 1] = (early_count + GROUP - 1) // GROUP
    order_ref[elements + 2] = (late_count + GROUP - 1) // GROUP


def local_part(a_strips, p_strips, nbr_local, ap_slot, slots, ghosts):
    elements, kb, _ = a_strips.shape
    blocks, pieces = ap_slot.shape[1:]
    kc = p_strips.shape[2] // pieces
    capacity = elements * (blocks - 1) + GROUP
    sums = pltpu.VMEM((elements * (slots + 1), kb, 2 * kc), jnp.float32)
    return pl.pallas_call(
        functools.partial(local_kernel, ghosts, slots),
        out_shape=[
            sums,
            sums,
            pltpu.VMEM((2 * capacity, kb, kb), jnp.bfloat16),
            pltpu.VMEM((elements, pieces * kc // 2, 2 * kb), jnp.bfloat16),
            jax.ShapeDtypeStruct((2 * capacity * (pieces + 1),), jnp.int32),
            jax.ShapeDtypeStruct((elements + 3,), jnp.int32),
        ],
        in_specs=[SMEM, SMEM, VMEM, VMEM],
        out_specs=[VMEM] * 4 + [SMEM] * 2,
        scratch_shapes=[pltpu.SMEM((8 * ghosts,), jnp.int32)],
        compiler_params=PARAMS,
        cost_estimate=pl.CostEstimate(flops=5 * 10**9, bytes_accessed=10**7, transcendentals=0),
        name="local_part",
    )(nbr_local.T, ap_slot.transpose(1, 2, 0), a_strips, p_strips)


def finish_kernel(late, info_ref, order_ref, tile_ref, ga_ref, pt_ref, *rest):
    parts = LATE if late else EARLY
    arrived, rest = rest[: len(parts)], rest[len(parts) :]
    rest = rest[2 + SUMS * late :]
    even_ref, odd_ref, *tiles = rest[: 2 + SUMS]
    sent, ghost_ref = rest[2 + SUMS : -1], rest[-1]
    pieces, slots, elements = tile_ref.shape
    kb, kc2 = even_ref.shape[1:]
    half = kc2 // 4
    stride = slots + 1
    ghosts = ghost_ref.shape[0] // 8
    first = ga_ref.shape[0] // 2 if late else 0
    offset = pair_offset()
    for part, ref in zip(parts, arrived):
        for at, cell in enumerate(arrived_cells(offset)[part]):
            rows = pl.ds(neighbour_of(cell) * ghosts, ghosts)
            ghost_ref[rows] = ref[at * ghosts : (at + 1) * ghosts]
    if not late:
        for ref in tiles:
            ref[...] = jnp.zeros_like(ref)
    left = lax.broadcasted_iota(jnp.int32, (kb, kc2), 1) < kc2 // 2

    def ghost_group(i, carry):
        for u in range(GROUP):
            at = first + i * GROUP + u
            product = jnp.dot(
                ga_ref[at],
                ghost_ref[info_ref[at * (pieces + 1) + pieces]],
                preferred_element_type=jnp.float32,
            )
            for k in range(pieces):
                ref = odd_ref if k % 2 else even_ref
                ref[info_ref[at * (pieces + 1) + k]] += product[
                    :, (k // 2) * kc2 : (k // 2 + 1) * kc2
                ]
        return carry

    lax.fori_loop(0, order_ref[elements + 1 + late], ghost_group, 0)
    zero = jnp.zeros((kb, kc2), jnp.bfloat16)

    def one(e):
        pt = pt_ref[e]
        for pair in range(slots // 2):
            columns = []
            for q in (2 * pair, 2 * pair + 1):
                x = jnp.where(left, even_ref[e * stride + q], odd_ref[e * stride + q])
                y = (x + pltpu.roll(x, kc2 // 2, 1)).astype(jnp.bfloat16)
                columns.append(
                    jnp.concatenate([jnp.where(left, y, zero), jnp.where(left, zero, y)], axis=0)
                )
            terms = jnp.dot(
                pt, jnp.concatenate(columns, axis=1), preferred_element_type=jnp.float32
            )
            for k in range(pieces):
                for u in range(2):
                    ref = tiles[(2 * k + u) % SUMS]
                    ref[tile_ref[k, 2 * pair + u, e]] += terms[
                        k * half : (k + 1) * half, u * kc2 : (u + 1) * kc2
                    ]

    def step(i, carry):
        for u in range(STEP):
            one(order_ref[i * STEP + u])
        return carry

    early_steps = order_ref[elements]
    if not late:
        lax.fori_loop(0, early_steps, step, 0)
        return
    lax.fori_loop(early_steps, elements // STEP, step, 0)
    capacity = sent[-1].shape[0]

    def total(cell):
        rows = pl.ds(cell * capacity, capacity)
        return functools.reduce(jnp.add, [ref[rows] for ref in tiles])

    for out, cells in zip(sent, sent_cells(offset)):
        for at, cell in enumerate(cells):
            out[at * capacity : (at + 1) * capacity] = total(cell).astype(out.dtype)
    sent[-1][...] = total(4)


def finish(late, info, order, tile_slot, ga, pt, arrived, sums, tiles_total):
    parts = LATE if late else EARLY
    kb, kc2 = sums[0].shape[1:]
    half = kc2 // 4
    capacity = tiles_total // 9
    out_shape = [pltpu.VMEM(x.shape, x.dtype) for x in sums[:2]]
    out_shape += [pltpu.VMEM((tiles_total, half, kc2), jnp.float32)] * SUMS
    if late:
        out_shape += [
            pltpu.VMEM((len(cells) * capacity, half, kc2), jnp.bfloat16) for cells in sent_cells(1)
        ]
        out_shape += [pltpu.VMEM((capacity, half, kc2), jnp.float32)]
    ghost = arrived[0].shape[1:]
    inputs = 5 + len(parts)
    return pl.pallas_call(
        functools.partial(finish_kernel, late),
        out_shape=out_shape,
        in_specs=[SMEM] * 3 + [VMEM] * (2 + len(parts) + len(sums)),
        out_specs=[VMEM] * len(out_shape),
        scratch_shapes=[pltpu.VMEM((8 * (arrived[4].shape[0]),) + ghost, jnp.bfloat16)],
        input_output_aliases={inputs + i: i for i in range(len(sums))},
        compiler_params=PARAMS,
        cost_estimate=pl.CostEstimate(flops=2 * 10**9, bytes_accessed=10**6, transcendentals=0),
        name="late_part" if late else "early_part",
    )(
        info,
        order,
        tile_slot.transpose(1, 2, 0),
        resident(ga),
        resident(pt),
        *(resident(arrived[part]) for part in parts),
        *sums,
    )


def owner_kernel(owner_ref, *rest):
    own, parcels, out_ref, tiles_ref = rest[0], rest[1:-2], rest[-2], rest[-1]
    tiles_ref[...] = jnp.zeros_like(tiles_ref)
    owned, half, kc2 = tiles_ref.shape
    capacity = own.shape[0]

    def add(cell, parcel, at):
        for g in range(capacity):
            tiles_ref[owner_ref[0, cell * capacity + g]] += parcel[at * capacity + g].astype(
                jnp.float32
            )

    add(4, own, 0)
    for parcel, cells in zip(parcels, arrived_cells(pair_offset())):
        for at, cell in enumerate(cells):
            add(cell, parcel, at)
    left = lax.broadcasted_iota(jnp.int32, (half, kc2), 1) < kc2 // 2
    for i in range(owned // 2):
        first, second = tiles_ref[2 * i], tiles_ref[2 * i + 1]
        columns = pl.ds(i * kc2, kc2)
        out_ref[:half, columns] = jnp.where(left, first, pltpu.roll(second, kc2 // 2, 1))
        out_ref[half:, columns] = jnp.where(left, pltpu.roll(first, kc2 // 2, 1), second)


def owner_sums(owner_map, own, parcels):
    _, half, kc2 = own.shape
    return pl.pallas_call(
        owner_kernel,
        out_shape=jax.ShapeDtypeStruct((2 * half, OWN * kc2 // 2), jnp.float32),
        in_specs=[SMEM] + [VMEM] * (1 + len(parcels)),
        out_specs=VMEM,
        scratch_shapes=[pltpu.VMEM((OWN, half, kc2), jnp.float32)],
        compiler_params=PARAMS,
        name="owner_sums",
    )(owner_map, resident(own), *map(resident, parcels))


def body(a_strips, p_strips, nbr_local, ap_slot, tile_slot, send_rows, owner_map):
    tiles_total = owner_map.shape[1]

    def beside(nbr):
        *results, order = local_part(
            a_strips, p_strips, nbr, ap_slot, tile_slot.shape[2], send_rows.shape[2]
        )
        return results, order

    (*sums, ga, pt, info, order), arrived = exchange(pack(send_rows, p_strips), nbr_local, beside)
    sums = finish(False, info, order, tile_slot, ga, pt, arrived, sums, tiles_total)
    results = finish(True, info, order, tile_slot, ga, pt, arrived, sums, tiles_total)
    *parcels, own = results[2 + SUMS :]
    return owner_sums(owner_map, own, exchange(parcels)[1])


def solution(mesh):
    placed = (
        P(("dom", "grp"), None, None),
        P(("dom", "grp"), None, None),
        P(("dom", "grp"), None),
        P(("dom", "grp"), None, None),
        P(("dom", "grp"), None, None),
        P(("dom", "grp"), None, None),
        P(("dom", "grp"), None),
    )
    return jax.shard_map(
        body, mesh=mesh, in_specs=placed, out_specs=P(None, ("dom", "grp")), check_vma=False
    )
```

```python
import functools

import jax
import jax.numpy as jnp
from jax import lax
from jax.experimental import pallas as pl
from jax.experimental.pallas import tpu as pltpu
from jax.sharding import PartitionSpec as P

OWN = 128
GROUP = 4
STEP = 4
SUMS = 4
OWNER_SUMS = 1
SMEM = pl.BlockSpec(memory_space=pltpu.SMEM)
VMEM = pl.BlockSpec(memory_space=pltpu.VMEM)
HBM = pl.BlockSpec(memory_space=pltpu.HBM)
PARAMS = pltpu.CompilerParams(vmem_limit_bytes=8 * 1024 * 1024)


def moved(x, a, along):
    domains, groups = lax.axis_size("dom"), lax.axis_size("grp")

    def target(j):
        if along == "pair":
            return j ^ 1
        if along == "far":
            return (j - 1 + 2 * (j % 2)) % groups
        return j

    pairs = [
        (i * groups + j, (i + a) % domains * groups + target(j))
        for i in range(domains)
        for j in range(groups)
    ]
    return lax.ppermute(x, ("dom", "grp"), pairs)


def resident(x):
    return pltpu.with_memory_space_constraint(x, pltpu.VMEM)


def exchange_rows(parts, nbr_local, local_work):
    pair, far, up, down = parts
    size = up.shape[0]
    pair, far = moved(pair, 0, "pair"), moved(far, 0, "far")
    up, down = jnp.concatenate([up, pair[size : 2 * size]]), jnp.concatenate([down, pair[2 * size :]])
    up, down, nbr_local = lax.optimization_barrier((up, down, nbr_local))
    *results, small = local_work(nbr_local)
    far, small = lax.optimization_barrier((far, small))
    up, down = moved(up, 1, "own"), moved(down, -1, "own")
    up_far = moved(far[size : 2 * size], 1, "own")
    down_far = moved(far[2 * size :], -1, "own")
    return (*results, small), (pair, far, up, down, up_far, down_far)


def exchange_tiles(parts, owner_map, first_sums):
    pair, far, up, down, up_far, down_far = parts
    size = up.shape[0]
    pair = moved(pair, 0, "pair")
    up_far, down_far = moved(up_far, 1, "own"), moved(down_far, -1, "own")
    up, down = jnp.concatenate([up, pair[size : 2 * size]]), jnp.concatenate([down, pair[2 * size :]])
    up, down, owner_map = lax.optimization_barrier((up, down, owner_map))
    sums, small = first_sums(pair, owner_map)
    up_far, down_far, small = lax.optimization_barrier((up_far, down_far, small))
    far = moved(jnp.concatenate([far, up_far, down_far]), 0, "far")
    return (*sums, small), (far, moved(up, 1, "own"), moved(down, -1, "own"))


def pair_offset():
    return 1 - 2 * (lax.axis_index("grp") % 2)


def sent_rows(offset):
    return (4 + offset, 7 + offset, 1 + offset), (4 - offset, 7 - offset, 1 - offset), (7,), (1,)


def arrived_rows(offset):
    return (4 + offset,), (4 - offset,), (1, 1 + offset), (7, 7 + offset), (1 - offset,), (7 - offset,)


def sent_tiles(offset):
    return (4 + offset, 7 + offset, 1 + offset), (4 - offset,), (7,), (1,), (7 - offset,), (1 - offset,)


def arrived_tiles(offset):
    return (4 - offset, 1 - offset, 7 - offset), (1, 1 + offset), (7, 7 + offset)


STAGES = ((0, 1), (2, 3), (4, 5))


def neighbour_of(cell):
    return cell - jnp.where(cell > 4, 1, 0)


def pack_kernel(send_hbm, p_hbm, *rest):
    outs, (send_ref, p_ref, sems) = rest[:-3], rest[-3:]
    ghosts = send_ref.shape[0]
    copies = [
        pltpu.make_async_copy(send_hbm, send_ref, sems.at[0]),
        pltpu.make_async_copy(p_hbm, p_ref, sems.at[1]),
    ]
    for copy in copies:
        copy.start()
    for copy in copies:
        copy.wait()
    for out, cells in zip(outs, sent_rows(pair_offset())):
        for at, cell in enumerate(cells):
            p = neighbour_of(cell)
            for g in range(ghosts):
                out[at * ghosts + g] = p_ref[send_ref[g, 0, p]]


def pack(send_rows, p_strips):
    ghosts = send_rows.shape[2]
    send = send_rows.transpose(2, 0, 1)
    return pl.pallas_call(
        pack_kernel,
        out_shape=[
            pltpu.VMEM((len(cells) * ghosts,) + p_strips.shape[1:], p_strips.dtype)
            for cells in sent_rows(1)
        ],
        in_specs=[HBM, HBM],
        out_specs=[VMEM] * 4,
        scratch_shapes=[
            pltpu.SMEM(send.shape, jnp.int32),
            pltpu.VMEM(p_strips.shape, p_strips.dtype),
            pltpu.SemaphoreType.DMA((2,)),
        ],
        compiler_params=PARAMS,
        name="pack",
    )(
        pltpu.with_memory_space_constraint(send, pltpu.HBM),
        pltpu.with_memory_space_constraint(p_strips, pltpu.HBM),
    )


def local_kernel(ghosts, slots, nbr_ref, ap_ref, a_ref, p_ref, *rest):
    even_ref, odd_ref, ga_ref, pt_ref, info_ref, order_ref, stage_ref, middle_ref = rest
    blocks, pieces, elements = ap_ref.shape
    kb = a_ref.shape[1]
    kc = p_ref.shape[2] // pieces
    stride = slots + 1
    stages = len(STAGES)
    capacity = ga_ref.shape[0]
    offset = pair_offset()
    for cell in (0, 1, 2, 3, 5, 6, 7, 8):
        stage = jnp.int32(cell // 3 != 1)
        if cell // 3 != 1 and cell % 3 != 1:
            stage = 1 + (cell % 3 - 1 == -offset).astype(jnp.int32)
        for g in range(ghosts):
            stage_ref[(cell - (cell > 4)) * ghosts + g] = stage

    def element(e, carry):
        counts, members = list(carry[:stages]), list(carry[stages:])
        for ref in (even_ref, odd_ref):
            ref[pl.ds(e * stride, stride)] = jnp.zeros((stride,) + ref.shape[1:], jnp.float32)
        last = jnp.int32(0)
        for j in range(blocks):
            n = nbr_ref[j, e]
            ghost = n >= elements
            a = a_ref[e, :, j * kb : (j + 1) * kb]
            product = jnp.dot(
                a, p_ref[jnp.where(ghost, 0, n)], preferred_element_type=jnp.float32
            )
            for k in range(pieces):
                row = e * stride + jnp.where(ghost, slots, ap_ref[j, k, e])
                piece = product[:, (k // 2) * 2 * kc : (k // 2 + 1) * 2 * kc]
                ref = odd_ref if k % 2 else even_ref
                ref[row] += piece
            if j > 0:
                stage = jnp.where(ghost, stage_ref[jnp.where(ghost, n - elements, 0)], 0)
                at = counts[0]
                for s in range(1, stages):
                    at = jnp.where(stage == s, s * capacity + counts[s], at)
                for k in range(pieces):
                    info_ref[at * (pieces + 2) + k] = e * stride + ap_ref[j, k, e]
                info_ref[at * (pieces + 2) + pieces] = n - elements
                listed = sum(counts)
                info_ref[at * (pieces + 2) + pieces + 1] = listed
                ga_ref[listed] = a
                for s in range(stages):
                    counts[s] += (ghost & (stage == s)).astype(jnp.int32)
                last = jnp.maximum(last, stage)
        first, middle, final = members
        order_ref[jnp.where(last == 2, elements - 1 - final, first)] = e
        middle_ref[middle] = e
        for s in range(stages):
            members[s] += (last == s).astype(jnp.int32)
        pt = p_ref[e].astype(jnp.float32).T.reshape(pieces, 2, kc // 2, kb)
        pt_ref[e, :, :kb] = pt[:, 0].reshape(pieces * kc // 2, kb).astype(jnp.bfloat16)
        pt_ref[e, :, kb:] = pt[:, 1].reshape(pieces * kc // 2, kb).astype(jnp.bfloat16)
        return *counts, *members

    totals = lax.fori_loop(0, elements, element, (jnp.int32(0),) * (2 * stages))
    counts, (first, middle, _) = totals[:stages], totals[stages:]

    def place(i, carry):
        order_ref[first + i] = middle_ref[i]
        return carry

    lax.fori_loop(0, middle, place, 0)
    for s in range(stages):
        for u in range(GROUP):
            at = s * capacity + counts[s] + u
            for k in range(pieces):
                info_ref[at * (pieces + 2) + k] = slots
            info_ref[at * (pieces + 2) + pieces] = 0
            info_ref[at * (pieces + 2) + pieces + 1] = 0
        order_ref[elements + s] = (counts[s] + GROUP - 1) // GROUP
    order_ref[elements + stages] = 0
    order_ref[elements + stages + 1] = first // STEP
    order_ref[elements + stages + 2] = (first + middle) // STEP
    order_ref[elements + stages + 3] = elements // STEP


def local_part(a_strips, p_strips, nbr_local, ap_slot, slots, ghosts):
    elements, kb, _ = a_strips.shape
    blocks, pieces = ap_slot.shape[1:]
    kc = p_strips.shape[2] // pieces
    capacity = elements * (blocks - 1) + GROUP
    sums = pltpu.VMEM((elements * (slots + 1), kb, 2 * kc), jnp.float32)
    return pl.pallas_call(
        functools.partial(local_kernel, ghosts, slots),
        out_shape=[
            sums,
            sums,
            pltpu.VMEM((capacity, kb, kb), jnp.bfloat16),
            pltpu.VMEM((elements, pieces * kc // 2, 2 * kb), jnp.bfloat16),
            jax.ShapeDtypeStruct((len(STAGES) * capacity * (pieces + 2),), jnp.int32),
            jax.ShapeDtypeStruct((elements + 2 * len(STAGES) + 1,), jnp.int32),
        ],
        in_specs=[SMEM, SMEM, VMEM, VMEM],
        out_specs=[VMEM] * 4 + [SMEM] * 2,
        scratch_shapes=[pltpu.SMEM((8 * ghosts,), jnp.int32), pltpu.SMEM((elements + 1,), jnp.int32)],
        compiler_params=PARAMS,
        cost_estimate=pl.CostEstimate(flops=5 * 10**9, bytes_accessed=10**7, transcendentals=0),
        name="local_part",
    )(nbr_local.T, ap_slot.transpose(1, 2, 0), a_strips, p_strips)


def finish_kernel(stage, info_ref, order_ref, tile_ref, ga_ref, pt_ref, *rest):
    parts = STAGES[stage]
    stages = len(STAGES)
    arrived, rest = rest[: len(parts)], rest[len(parts) :]
    rest = rest[2 + SUMS * (stage > 0) :]
    even_ref, odd_ref, *tiles = rest[: 2 + SUMS]
    sent, ghost_ref = rest[2 + SUMS : -1], rest[-1]
    pieces, slots, elements = tile_ref.shape
    kb, kc2 = even_ref.shape[1:]
    half = kc2 // 4
    stride = slots + 1
    ghosts = ghost_ref.shape[0] // 8
    first = ga_ref.shape[0] * stage
    offset = pair_offset()
    for part, ref in zip(parts, arrived):
        for at, cell in enumerate(arrived_rows(offset)[part]):
            rows = pl.ds(neighbour_of(cell) * ghosts, ghosts)
            ghost_ref[rows] = ref[at * ghosts : (at + 1) * ghosts]
    if stage == 0:
        for ref in tiles:
            ref[...] = jnp.zeros_like(ref)
    left = lax.broadcasted_iota(jnp.int32, (kb, kc2), 1) < kc2 // 2

    def ghost_group(i, carry):
        for u in range(GROUP):
            at = first + i * GROUP + u
            product = jnp.dot(
                ga_ref[info_ref[at * (pieces + 2) + pieces + 1]],
                ghost_ref[info_ref[at * (pieces + 2) + pieces]],
                preferred_element_type=jnp.float32,
            )
            for k in range(pieces):
                ref = odd_ref if k % 2 else even_ref
                ref[info_ref[at * (pieces + 2) + k]] += product[
                    :, (k // 2) * kc2 : (k // 2 + 1) * kc2
                ]
        return carry

    lax.fori_loop(0, order_ref[elements + stage], ghost_group, 0)
    zero = jnp.zeros((kb, kc2), jnp.bfloat16)

    def one(e):
        pt = pt_ref[e]
        for pair in range(slots // 2):
            columns = []
            for q in (2 * pair, 2 * pair + 1):
                x = jnp.where(left, even_ref[e * stride + q], odd_ref[e * stride + q])
                y = (x + pltpu.roll(x, kc2 // 2, 1)).astype(jnp.bfloat16)
                columns.append(
                    jnp.concatenate([jnp.where(left, y, zero), jnp.where(left, zero, y)], axis=0)
                )
            terms = jnp.dot(
                pt, jnp.concatenate(columns, axis=1), preferred_element_type=jnp.float32
            )
            for k in range(pieces):
                for u in range(2):
                    ref = tiles[(2 * k + u) % SUMS]
                    ref[tile_ref[k, 2 * pair + u, e]] += terms[
                        k * half : (k + 1) * half, u * kc2 : (u + 1) * kc2
                    ]

    def step(i, carry):
        for u in range(STEP):
            one(order_ref[i * STEP + u])
        return carry

    begin = elements + stages + stage
    lax.fori_loop(order_ref[begin], order_ref[begin + 1], step, 0)
    if stage < stages - 1:
        return
    capacity = sent[-1].shape[0]

    def total(cell):
        rows = pl.ds(cell * capacity, capacity)
        return functools.reduce(jnp.add, [ref[rows] for ref in tiles])

    for out, cells in zip(sent, sent_tiles(offset)):
        for at, cell in enumerate(cells):
            out[at * capacity : (at + 1) * capacity] = total(cell).astype(out.dtype)
    sent[-1][...] = total(4)


def finish(stage, info, order, tile_slot, ga, pt, arrived, sums, tiles_total):
    parts = STAGES[stage]
    kb, kc2 = sums[0].shape[1:]
    half = kc2 // 4
    capacity = tiles_total // 9
    out_shape = [pltpu.VMEM(x.shape, x.dtype) for x in sums[:2]]
    out_shape += [pltpu.VMEM((tiles_total, half, kc2), jnp.float32)] * SUMS
    if stage == len(STAGES) - 1:
        out_shape += [
            pltpu.VMEM((len(cells) * capacity, half, kc2), jnp.bfloat16) for cells in sent_tiles(1)
        ]
        out_shape += [pltpu.VMEM((capacity, half, kc2), jnp.float32)]
    inputs = 5 + len(parts)
    return pl.pallas_call(
        functools.partial(finish_kernel, stage),
        out_shape=out_shape,
        in_specs=[SMEM] * 3 + [VMEM] * (2 + len(parts) + len(sums)),
        out_specs=[VMEM] * len(out_shape),
        scratch_shapes=[
            pltpu.VMEM((8 * arrived[4].shape[0],) + arrived[4].shape[1:], jnp.bfloat16)
        ],
        input_output_aliases={inputs + i: i for i in range(len(sums))},
        compiler_params=PARAMS,
        cost_estimate=pl.CostEstimate(flops=2 * 10**9, bytes_accessed=10**6, transcendentals=0),
        name=("first_part", "middle_part", "last_part")[stage],
    )(
        info,
        order,
        tile_slot.transpose(1, 2, 0),
        resident(ga),
        resident(pt),
        *(resident(arrived[part]) for part in parts),
        *sums,
    )


def add_tiles(owner_ref, sums, cell, parcel, at, capacity):
    for g in range(capacity):
        ref = sums[g % len(sums)]
        ref[owner_ref[0, cell * capacity + g]] += parcel[at * capacity + g].astype(jnp.float32)


def first_sums_kernel(owner_ref, own, pair, *rest):
    sums, small = rest[:-1], rest[-1]
    for ref in sums:
        ref[...] = jnp.zeros_like(ref)
    capacity = own.shape[0]
    add_tiles(owner_ref, sums, 4, own, 0, capacity)
    add_tiles(owner_ref, sums, 4 + pair_offset(), pair, 0, capacity)
    small[...] = jnp.zeros_like(small)


def first_sums(own, pair, owner_map):
    _, half, kc2 = own.shape
    *sums, small = pl.pallas_call(
        first_sums_kernel,
        out_shape=[pltpu.VMEM((OWN, half, kc2), jnp.float32)] * OWNER_SUMS
        + [jax.ShapeDtypeStruct((8, 128), jnp.float32)],
        in_specs=[SMEM, VMEM, VMEM],
        out_specs=[VMEM] * (OWNER_SUMS + 1),
        compiler_params=PARAMS,
        cost_estimate=pl.CostEstimate(flops=10**9, bytes_accessed=10**6, transcendentals=0),
        name="first_sums",
    )(owner_map, resident(own), resident(pair))
    return sums, small


def more_sums_kernel(owner_ref, up, down, *rest):
    sums = rest[-OWNER_SUMS:]
    capacity = owner_ref.shape[1] // 9
    for parcel, cells in zip((up, down), arrived_tiles(pair_offset())[1:]):
        for at, cell in enumerate(cells):
            add_tiles(owner_ref, sums, cell, parcel, at, capacity)


def more_sums(owner_map, sums, up, down):
    return pl.pallas_call(
        more_sums_kernel,
        out_shape=[pltpu.VMEM(x.shape, x.dtype) for x in sums],
        in_specs=[SMEM] + [VMEM] * (2 + len(sums)),
        out_specs=[VMEM] * len(sums),
        input_output_aliases={3 + i: i for i in range(len(sums))},
        compiler_params=PARAMS,
        cost_estimate=pl.CostEstimate(flops=10**9, bytes_accessed=10**6, transcendentals=0),
        name="more_sums",
    )(owner_map, resident(up), resident(down), *sums)


def owner_kernel(owner_ref, far, *rest):
    sums, (out_ref, stage_ref, sems) = rest[-3 - OWNER_SUMS : -3], rest[-3:]
    capacity = owner_ref.shape[1] // 9
    for at, cell in enumerate(arrived_tiles(pair_offset())[0]):
        add_tiles(owner_ref, sums, cell, far, at, capacity)
    owned, half, kc2 = sums[0].shape
    left = lax.broadcasted_iota(jnp.int32, (8, kc2), 1) < kc2 // 2
    copies = []
    for row in range(0, half, 8):
        for i in range(owned // 2):
            first = functools.reduce(jnp.add, [ref[2 * i, row : row + 8] for ref in sums])
            second = functools.reduce(jnp.add, [ref[2 * i + 1, row : row + 8] for ref in sums])
            columns = pl.ds(i * kc2, kc2)
            stage_ref[row : row + 8, columns] = jnp.where(
                left, first, pltpu.roll(second, kc2 // 2, 1)
            )
            stage_ref[half + row : half + row + 8, columns] = jnp.where(
                left, pltpu.roll(first, kc2 // 2, 1), second
            )
        for at in (row, half + row):
            rows = pl.ds(at, 8)
            copies.append(
                pltpu.make_async_copy(stage_ref.at[rows], out_ref.at[rows], sems.at[len(copies)])
            )
            copies[-1].start()
    for copy in copies:
        copy.wait()


def owner_sums(owner_map, sums, small, far):
    _, half, kc2 = sums[0].shape
    out = jax.ShapeDtypeStruct((2 * half, OWN * kc2 // 2), jnp.float32)
    results = pl.pallas_call(
        owner_kernel,
        out_shape=[pltpu.VMEM(x.shape, x.dtype) for x in sums] + [out],
        in_specs=[SMEM] + [VMEM] * (1 + len(sums)) + [HBM],
        out_specs=[VMEM] * len(sums) + [HBM],
        scratch_shapes=[
            pltpu.VMEM(out.shape, out.dtype),
            pltpu.SemaphoreType.DMA((2 * half // 8,)),
        ],
        input_output_aliases={2 + i: i for i in range(len(sums))},
        compiler_params=PARAMS,
        name="owner_sums",
    )(owner_map, resident(far), *sums, small)
    return results[-1]


def body(a_strips, p_strips, nbr_local, ap_slot, tile_slot, send_rows, owner_map):
    tiles_total = owner_map.shape[1]

    def local_work(nbr):
        return local_part(
            a_strips, p_strips, nbr, ap_slot, tile_slot.shape[2], send_rows.shape[2]
        )

    (*sums, ga, pt, info, order), arrived = exchange_rows(
        pack(send_rows, p_strips), nbr_local, local_work
    )
    for stage in range(len(STAGES)):
        sums = finish(stage, info, order, tile_slot, ga, pt, arrived, sums, tiles_total)
    *parcels, own = sums[2 + SUMS :]
    (*sums, small), (far, up, down) = exchange_tiles(
        parcels, owner_map, functools.partial(first_sums, own)
    )
    sums = more_sums(owner_map, sums, up, down)
    return owner_sums(owner_map, sums, small, far)


def solution(mesh):
    placed = (
        P(("dom", "grp"), None, None),
        P(("dom", "grp"), None, None),
        P(("dom", "grp"), None),
        P(("dom", "grp"), None, None),
        P(("dom", "grp"), None, None),
        P(("dom", "grp"), None, None),
        P(("dom", "grp"), None),
    )
    return jax.shard_map(
        body, mesh=mesh, in_specs=placed, out_specs=P(None, ("dom", "grp")), check_vma=False
    )
```

```python
import functools

import jax
import jax.numpy as jnp
from jax import lax
from jax.experimental import pallas as pl
from jax.experimental.pallas import tpu as pltpu
from jax.sharding import PartitionSpec as P

OWN = 128
GROUP = 4
STEP = 4
SUMS = 4
OWNER_SUMS = 1
SMEM = pl.BlockSpec(memory_space=pltpu.SMEM)
VMEM = pl.BlockSpec(memory_space=pltpu.VMEM)
HBM = pl.BlockSpec(memory_space=pltpu.HBM)
PARAMS = pltpu.CompilerParams(vmem_limit_bytes=8 * 1024 * 1024)


def moved(x, a, along):
    domains, groups = lax.axis_size("dom"), lax.axis_size("grp")

    def target(j):
        if along == "pair":
            return j ^ 1
        if along == "far":
            return (j - 1 + 2 * (j % 2)) % groups
        return j

    pairs = [
        (i * groups + j, (i + a) % domains * groups + target(j))
        for i in range(domains)
        for j in range(groups)
    ]
    return lax.ppermute(x, ("dom", "grp"), pairs)


def resident(x):
    return pltpu.with_memory_space_constraint(x, pltpu.VMEM)


def exchange_rows(parts, nbr_local, local_work):
    pair, far, up, down = parts
    size = up.shape[0]
    pair, far = moved(pair, 0, "pair"), moved(far, 0, "far")
    up, down = jnp.concatenate([up, pair[size : 2 * size]]), jnp.concatenate([down, pair[2 * size :]])
    up, down, nbr_local = lax.optimization_barrier((up, down, nbr_local))
    *results, small = local_work(nbr_local)
    far, small = lax.optimization_barrier((far, small))
    up, down = moved(up, 1, "own"), moved(down, -1, "own")
    up_far = moved(far[size : 2 * size], 1, "own")
    down_far = moved(far[2 * size :], -1, "own")
    return (*results, small), (pair, far, up, down, up_far, down_far)


def exchange_tiles(parts, first_sums):
    up, down, far, up_far, down_far, pair = parts
    size = pair.shape[0]
    up, down, far = moved(up, 1, "own"), moved(down, -1, "own"), moved(far, 0, "far")
    up_far, down_far = moved(up_far, 1, "far"), moved(down_far, -1, "far")
    sums, small = first_sums()
    up, down, small = lax.optimization_barrier((up, down, small))
    pair = moved(jnp.concatenate([pair, up[size:], down[size:]]), 0, "pair")
    return sums, small, (up, down, far, up_far, down_far, pair)


def pair_offset():
    return 1 - 2 * (lax.axis_index("grp") % 2)


def sent_rows(offset):
    return (4 + offset, 7 + offset, 1 + offset), (4 - offset, 7 - offset, 1 - offset), (7,), (1,)


def arrived_rows(offset):
    return (4 + offset,), (4 - offset,), (1, 1 + offset), (7, 7 + offset), (1 - offset,), (7 - offset,)


def sent_tiles(offset):
    return (7, 7 + offset), (1, 1 + offset), (4 - offset,), (7 - offset,), (1 - offset,), (4 + offset,)


def arrived_tiles(offset):
    return (1,), (7,), (4 - offset,), (1 - offset,), (7 - offset,), (4 + offset, 1 + offset, 7 + offset)


STAGES = ((0, 1), (2, 3), (4, 5))


def neighbour_of(cell):
    return cell - jnp.where(cell > 4, 1, 0)


def pack_kernel(send_hbm, p_hbm, *rest):
    outs, (send_ref, p_ref, sems) = rest[:-3], rest[-3:]
    ghosts = send_ref.shape[0]
    copies = [
        pltpu.make_async_copy(send_hbm, send_ref, sems.at[0]),
        pltpu.make_async_copy(p_hbm, p_ref, sems.at[1]),
    ]
    for copy in copies:
        copy.start()
    for copy in copies:
        copy.wait()
    for out, cells in zip(outs, sent_rows(pair_offset())):
        for at, cell in enumerate(cells):
            p = neighbour_of(cell)
            for g in range(ghosts):
                out[at * ghosts + g] = p_ref[send_ref[g, 0, p]]


def pack(send_rows, p_strips):
    ghosts = send_rows.shape[2]
    send = send_rows.transpose(2, 0, 1)
    return pl.pallas_call(
        pack_kernel,
        out_shape=[
            pltpu.VMEM((len(cells) * ghosts,) + p_strips.shape[1:], p_strips.dtype)
            for cells in sent_rows(1)
        ],
        in_specs=[HBM, HBM],
        out_specs=[VMEM] * 4,
        scratch_shapes=[
            pltpu.SMEM(send.shape, jnp.int32),
            pltpu.VMEM(p_strips.shape, p_strips.dtype),
            pltpu.SemaphoreType.DMA((2,)),
        ],
        compiler_params=PARAMS,
        name="pack",
    )(
        pltpu.with_memory_space_constraint(send, pltpu.HBM),
        pltpu.with_memory_space_constraint(p_strips, pltpu.HBM),
    )


def local_kernel(ghosts, slots, nbr_ref, ap_ref, a_ref, p_ref, *rest):
    even_ref, odd_ref, ga_ref, pt_ref, info_ref, order_ref, stage_ref, middle_ref = rest
    blocks, pieces, elements = ap_ref.shape
    kb = a_ref.shape[1]
    kc = p_ref.shape[2] // pieces
    stride = slots + 1
    stages = len(STAGES)
    capacity = ga_ref.shape[0]
    offset = pair_offset()
    for cell in (0, 1, 2, 3, 5, 6, 7, 8):
        stage = jnp.int32(cell // 3 != 1)
        if cell // 3 != 1 and cell % 3 != 1:
            stage = 1 + (cell % 3 - 1 == -offset).astype(jnp.int32)
        for g in range(ghosts):
            stage_ref[(cell - (cell > 4)) * ghosts + g] = stage

    def element(e, carry):
        counts, members = list(carry[:stages]), list(carry[stages:])
        for ref in (even_ref, odd_ref):
            ref[pl.ds(e * stride, stride)] = jnp.zeros((stride,) + ref.shape[1:], jnp.float32)
        last = jnp.int32(0)
        for j in range(blocks):
            n = nbr_ref[j, e]
            ghost = n >= elements
            a = a_ref[e, :, j * kb : (j + 1) * kb]
            product = jnp.dot(
                a, p_ref[jnp.where(ghost, 0, n)], preferred_element_type=jnp.float32
            )
            for k in range(pieces):
                row = e * stride + jnp.where(ghost, slots, ap_ref[j, k, e])
                piece = product[:, (k // 2) * 2 * kc : (k // 2 + 1) * 2 * kc]
                ref = odd_ref if k % 2 else even_ref
                ref[row] += piece
            if j > 0:
                stage = jnp.where(ghost, stage_ref[jnp.where(ghost, n - elements, 0)], 0)
                at = counts[0]
                for s in range(1, stages):
                    at = jnp.where(stage == s, s * capacity + counts[s], at)
                for k in range(pieces):
                    info_ref[at * (pieces + 2) + k] = e * stride + ap_ref[j, k, e]
                info_ref[at * (pieces + 2) + pieces] = n - elements
                listed = sum(counts)
                info_ref[at * (pieces + 2) + pieces + 1] = listed
                ga_ref[listed] = a
                for s in range(stages):
                    counts[s] += (ghost & (stage == s)).astype(jnp.int32)
                last = jnp.maximum(last, stage)
        first, middle, final = members
        order_ref[jnp.where(last == 2, elements - 1 - final, first)] = e
        middle_ref[middle] = e
        for s in range(stages):
            members[s] += (last == s).astype(jnp.int32)
        pt = p_ref[e].astype(jnp.float32).T.reshape(pieces, 2, kc // 2, kb)
        pt_ref[e, :, :kb] = pt[:, 0].reshape(pieces * kc // 2, kb).astype(jnp.bfloat16)
        pt_ref[e, :, kb:] = pt[:, 1].reshape(pieces * kc // 2, kb).astype(jnp.bfloat16)
        return *counts, *members

    totals = lax.fori_loop(0, elements, element, (jnp.int32(0),) * (2 * stages))
    counts, (first, middle, _) = totals[:stages], totals[stages:]

    def place(i, carry):
        order_ref[first + i] = middle_ref[i]
        return carry

    lax.fori_loop(0, middle, place, 0)
    for s in range(stages):
        for u in range(GROUP):
            at = s * capacity + counts[s] + u
            for k in range(pieces):
                info_ref[at * (pieces + 2) + k] = slots
            info_ref[at * (pieces + 2) + pieces] = 0
            info_ref[at * (pieces + 2) + pieces + 1] = 0
        order_ref[elements + s] = (counts[s] + GROUP - 1) // GROUP
    order_ref[elements + stages] = 0
    order_ref[elements + stages + 1] = first // STEP
    order_ref[elements + stages + 2] = (first + middle) // STEP
    order_ref[elements + stages + 3] = elements // STEP


def local_part(a_strips, p_strips, nbr_local, ap_slot, slots, ghosts):
    elements, kb, _ = a_strips.shape
    blocks, pieces = ap_slot.shape[1:]
    kc = p_strips.shape[2] // pieces
    capacity = elements * (blocks - 1) + GROUP
    sums = pltpu.VMEM((elements * (slots + 1), kb, 2 * kc), jnp.float32)
    return pl.pallas_call(
        functools.partial(local_kernel, ghosts, slots),
        out_shape=[
            sums,
            sums,
            pltpu.VMEM((capacity, kb, kb), jnp.bfloat16),
            pltpu.VMEM((elements, pieces * kc // 2, 2 * kb), jnp.bfloat16),
            jax.ShapeDtypeStruct((len(STAGES) * capacity * (pieces + 2),), jnp.int32),
            jax.ShapeDtypeStruct((elements + 2 * len(STAGES) + 1,), jnp.int32),
        ],
        in_specs=[SMEM, SMEM, VMEM, VMEM],
        out_specs=[VMEM] * 4 + [SMEM] * 2,
        scratch_shapes=[pltpu.SMEM((8 * ghosts,), jnp.int32), pltpu.SMEM((elements + 1,), jnp.int32)],
        compiler_params=PARAMS,
        cost_estimate=pl.CostEstimate(flops=5 * 10**9, bytes_accessed=10**7, transcendentals=0),
        name="local_part",
    )(nbr_local.T, ap_slot.transpose(1, 2, 0), a_strips, p_strips)


def finish_kernel(stage, info_ref, order_ref, tile_ref, ga_ref, pt_ref, *rest):
    parts = STAGES[stage]
    stages = len(STAGES)
    arrived, rest = rest[: len(parts)], rest[len(parts) :]
    rest = rest[2 + SUMS * (stage > 0) :]
    even_ref, odd_ref, *tiles = rest[: 2 + SUMS]
    sent, ghost_ref = rest[2 + SUMS : -1], rest[-1]
    pieces, slots, elements = tile_ref.shape
    kb, kc2 = even_ref.shape[1:]
    half = kc2 // 4
    stride = slots + 1
    ghosts = ghost_ref.shape[0] // 8
    first = ga_ref.shape[0] * stage
    offset = pair_offset()
    for part, ref in zip(parts, arrived):
        for at, cell in enumerate(arrived_rows(offset)[part]):
            rows = pl.ds(neighbour_of(cell) * ghosts, ghosts)
            ghost_ref[rows] = ref[at * ghosts : (at + 1) * ghosts]
    if stage == 0:
        for ref in tiles:
            ref[...] = jnp.zeros_like(ref)
    left = lax.broadcasted_iota(jnp.int32, (kb, kc2), 1) < kc2 // 2

    def ghost_group(i, carry):
        for u in range(GROUP):
            at = first + i * GROUP + u
            product = jnp.dot(
                ga_ref[info_ref[at * (pieces + 2) + pieces + 1]],
                ghost_ref[info_ref[at * (pieces + 2) + pieces]],
                preferred_element_type=jnp.float32,
            )
            for k in range(pieces):
                ref = odd_ref if k % 2 else even_ref
                ref[info_ref[at * (pieces + 2) + k]] += product[
                    :, (k // 2) * kc2 : (k // 2 + 1) * kc2
                ]
        return carry

    lax.fori_loop(0, order_ref[elements + stage], ghost_group, 0)
    zero = jnp.zeros((kb, kc2), jnp.bfloat16)

    def one(e):
        pt = pt_ref[e]
        for pair in range(slots // 2):
            columns = []
            for q in (2 * pair, 2 * pair + 1):
                x = jnp.where(left, even_ref[e * stride + q], odd_ref[e * stride + q])
                y = (x + pltpu.roll(x, kc2 // 2, 1)).astype(jnp.bfloat16)
                columns.append(
                    jnp.concatenate([jnp.where(left, y, zero), jnp.where(left, zero, y)], axis=0)
                )
            terms = jnp.dot(
                pt, jnp.concatenate(columns, axis=1), preferred_element_type=jnp.float32
            )
            for k in range(pieces):
                for u in range(2):
                    ref = tiles[(2 * k + u) % SUMS]
                    ref[tile_ref[k, 2 * pair + u, e]] += terms[
                        k * half : (k + 1) * half, u * kc2 : (u + 1) * kc2
                    ]

    def step(i, carry):
        for u in range(STEP):
            one(order_ref[i * STEP + u])
        return carry

    begin = elements + stages + stage
    lax.fori_loop(order_ref[begin], order_ref[begin + 1], step, 0)
    if stage < stages - 1:
        return
    capacity = sent[-1].shape[0]

    def total(cell):
        rows = pl.ds(cell * capacity, capacity)
        return functools.reduce(jnp.add, [ref[rows] for ref in tiles])

    for out, cells in zip(sent, sent_tiles(offset)):
        for at, cell in enumerate(cells):
            out[at * capacity : (at + 1) * capacity] = total(cell).astype(out.dtype)
    sent[-1][...] = total(4)


def finish(stage, info, order, tile_slot, ga, pt, arrived, sums, tiles_total):
    parts = STAGES[stage]
    kb, kc2 = sums[0].shape[1:]
    half = kc2 // 4
    capacity = tiles_total // 9
    out_shape = [pltpu.VMEM(x.shape, x.dtype) for x in sums[:2]]
    out_shape += [pltpu.VMEM((tiles_total, half, kc2), jnp.float32)] * SUMS
    if stage == len(STAGES) - 1:
        out_shape += [
            pltpu.VMEM((len(cells) * capacity, half, kc2), jnp.bfloat16) for cells in sent_tiles(1)
        ]
        out_shape += [pltpu.VMEM((capacity, half, kc2), jnp.float32)]
    inputs = 5 + len(parts)
    return pl.pallas_call(
        functools.partial(finish_kernel, stage),
        out_shape=out_shape,
        in_specs=[SMEM] * 3 + [VMEM] * (2 + len(parts) + len(sums)),
        out_specs=[VMEM] * len(out_shape),
        scratch_shapes=[
            pltpu.VMEM((8 * arrived[4].shape[0],) + arrived[4].shape[1:], jnp.bfloat16)
        ],
        input_output_aliases={inputs + i: i for i in range(len(sums))},
        compiler_params=PARAMS,
        cost_estimate=pl.CostEstimate(flops=2 * 10**9, bytes_accessed=10**6, transcendentals=0),
        name=("first_part", "middle_part", "last_part")[stage],
    )(
        info,
        order,
        tile_slot.transpose(1, 2, 0),
        resident(ga),
        resident(pt),
        *(resident(arrived[part]) for part in parts),
        *sums,
    )


def add_tiles(owner_ref, sums, cell, parcel, at, capacity):
    for g in range(capacity):
        ref = sums[g % len(sums)]
        ref[owner_ref[0, cell * capacity + g]] += parcel[at * capacity + g].astype(jnp.float32)


def first_sums_kernel(owner_ref, own, *rest):
    sums, small = rest[:-1], rest[-1]
    for ref in sums:
        ref[...] = jnp.zeros_like(ref)
    add_tiles(owner_ref, sums, 4, own, 0, own.shape[0])
    small[...] = jnp.zeros_like(small)


def first_sums(owner_map, own):
    _, half, kc2 = own.shape
    *sums, small = pl.pallas_call(
        first_sums_kernel,
        out_shape=[pltpu.VMEM((OWN, half, kc2), jnp.float32)] * OWNER_SUMS
        + [jax.ShapeDtypeStruct((8, 128), jnp.float32)],
        in_specs=[SMEM, VMEM],
        out_specs=[VMEM] * (OWNER_SUMS + 1),
        compiler_params=PARAMS,
        cost_estimate=pl.CostEstimate(flops=10**9, bytes_accessed=10**6, transcendentals=0),
        name="first_sums",
    )(owner_map, resident(own))
    return sums, small


def more_sums_kernel(owner_ref, *rest):
    arrived, sums = rest[: -2 * OWNER_SUMS], rest[-OWNER_SUMS:]
    capacity = owner_ref.shape[1] // 9
    for parcel, cells in zip(arrived, arrived_tiles(pair_offset())):
        add_tiles(owner_ref, sums, cells[0], parcel, 0, capacity)


def more_sums(owner_map, sums, arrived):
    inputs = 1 + len(arrived)
    return pl.pallas_call(
        more_sums_kernel,
        out_shape=[pltpu.VMEM(x.shape, x.dtype) for x in sums],
        in_specs=[SMEM] + [VMEM] * (len(arrived) + len(sums)),
        out_specs=[VMEM] * len(sums),
        input_output_aliases={inputs + i: i for i in range(len(sums))},
        compiler_params=PARAMS,
        cost_estimate=pl.CostEstimate(flops=2 * 10**10, bytes_accessed=10**6, transcendentals=0),
        name="more_sums",
    )(owner_map, *map(resident, arrived), *sums)


def owner_kernel(owner_ref, pair, *rest):
    sums, (out_ref, stage_ref, sems) = rest[-3 - OWNER_SUMS : -3], rest[-3:]
    capacity = owner_ref.shape[1] // 9
    for at, cell in enumerate(arrived_tiles(pair_offset())[-1]):
        add_tiles(owner_ref, sums, cell, pair, at, capacity)
    owned, half, kc2 = sums[0].shape
    left = lax.broadcasted_iota(jnp.int32, (8, kc2), 1) < kc2 // 2
    copies = []
    for row in range(0, half, 8):
        for i in range(owned // 2):
            first = functools.reduce(jnp.add, [ref[2 * i, row : row + 8] for ref in sums])
            second = functools.reduce(jnp.add, [ref[2 * i + 1, row : row + 8] for ref in sums])
            columns = pl.ds(i * kc2, kc2)
            stage_ref[row : row + 8, columns] = jnp.where(
                left, first, pltpu.roll(second, kc2 // 2, 1)
            )
            stage_ref[half + row : half + row + 8, columns] = jnp.where(
                left, pltpu.roll(first, kc2 // 2, 1), second
            )
        for at in (row, half + row):
            rows = pl.ds(at, 8)
            copies.append(
                pltpu.make_async_copy(stage_ref.at[rows], out_ref.at[rows], sems.at[len(copies)])
            )
            copies[-1].start()
    for copy in copies:
        copy.wait()


def owner_sums(owner_map, sums, small, pair):
    _, half, kc2 = sums[0].shape
    out = jax.ShapeDtypeStruct((2 * half, OWN * kc2 // 2), jnp.float32)
    results = pl.pallas_call(
        owner_kernel,
        out_shape=[pltpu.VMEM(x.shape, x.dtype) for x in sums] + [out],
        in_specs=[SMEM] + [VMEM] * (1 + len(sums)) + [HBM],
        out_specs=[VMEM] * len(sums) + [HBM],
        scratch_shapes=[
            pltpu.VMEM(out.shape, out.dtype),
            pltpu.SemaphoreType.DMA((2 * half // 8,)),
        ],
        input_output_aliases={2 + i: i for i in range(len(sums))},
        compiler_params=PARAMS,
        name="owner_sums",
    )(owner_map, resident(pair), *sums, small)
    return results[-1]


def body(a_strips, p_strips, nbr_local, ap_slot, tile_slot, send_rows, owner_map):
    tiles_total = owner_map.shape[1]

    def local_work(nbr):
        return local_part(
            a_strips, p_strips, nbr, ap_slot, tile_slot.shape[2], send_rows.shape[2]
        )

    (*sums, ga, pt, info, order), arrived = exchange_rows(
        pack(send_rows, p_strips), nbr_local, local_work
    )
    for stage in range(len(STAGES)):
        sums = finish(stage, info, order, tile_slot, ga, pt, arrived, sums, tiles_total)
    *parcels, own = sums[2 + SUMS :]
    sums, small, (*parcels, pair) = exchange_tiles(
        parcels, functools.partial(first_sums, owner_map, own)
    )
    sums = more_sums(owner_map, sums, parcels)
    return owner_sums(owner_map, sums, small, pair)


def solution(mesh):
    placed = (
        P(("dom", "grp"), None, None),
        P(("dom", "grp"), None, None),
        P(("dom", "grp"), None),
        P(("dom", "grp"), None, None),
        P(("dom", "grp"), None, None),
        P(("dom", "grp"), None, None),
        P(("dom", "grp"), None),
    )
    return jax.shard_map(
        body, mesh=mesh, in_specs=placed, out_specs=P(None, ("dom", "grp")), check_vma=False
    )
```

```python
import functools

import jax
import jax.numpy as jnp
from jax import lax
from jax.experimental import pallas as pl
from jax.experimental.pallas import tpu as pltpu
from jax.sharding import PartitionSpec as P

OWN = 128
GROUP = 12
STEP = 4
SUMS = 4
OWNER_SUMS = 1
SMEM = pl.BlockSpec(memory_space=pltpu.SMEM)
VMEM = pl.BlockSpec(memory_space=pltpu.VMEM)
HBM = pl.BlockSpec(memory_space=pltpu.HBM)
PARAMS = pltpu.CompilerParams(vmem_limit_bytes=8 * 1024 * 1024)


def moved(x, a, along):
    domains, groups = lax.axis_size("dom"), lax.axis_size("grp")

    def target(j):
        if along == "pair":
            return j ^ 1
        if along == "far":
            return (j - 1 + 2 * (j % 2)) % groups
        return j

    pairs = [
        (i * groups + j, (i + a) % domains * groups + target(j))
        for i in range(domains)
        for j in range(groups)
    ]
    return lax.ppermute(x, ("dom", "grp"), pairs)


def resident(x):
    return pltpu.with_memory_space_constraint(x, pltpu.VMEM)


def scalar(x):
    return pltpu.with_memory_space_constraint(x, pltpu.SMEM)


def exchange_rows(parts, nbr_local, local_work):
    pair, far, up, down = parts
    size = up.shape[0]
    pair, far = moved(pair, 0, "pair"), moved(far, 0, "far")
    up, down = jnp.concatenate([up, pair[size : 2 * size]]), jnp.concatenate([down, pair[2 * size :]])
    up, down, nbr_local = lax.optimization_barrier((up, down, nbr_local))
    *results, small = local_work(nbr_local)
    far, small = lax.optimization_barrier((far, small))
    up, down = moved(up, 1, "own"), moved(down, -1, "own")
    up_far = moved(far[size : 2 * size], 1, "own")
    down_far = moved(far[2 * size :], -1, "own")
    return (*results, small), (pair, far, up, down, up_far, down_far)


def exchange_tiles(parts, first_sums):
    up, down, far, up_far, down_far, pair = parts
    size = pair.shape[0]
    up, down, far = moved(up, 1, "own"), moved(down, -1, "own"), moved(far, 0, "far")
    sums, small = first_sums()
    up_far, down_far, small = lax.optimization_barrier((up_far, down_far, small))
    up_far, down_far = moved(up_far, 1, "far"), moved(down_far, -1, "far")
    up, down, small = lax.optimization_barrier((up, down, small))
    pair = moved(jnp.concatenate([pair, up[size:], down[size:]]), 0, "pair")
    return sums, small, (up, down, far, up_far, down_far, pair)


def pair_offset():
    return 1 - 2 * (lax.axis_index("grp") % 2)


def sent_rows(offset):
    return (4 + offset, 7 + offset, 1 + offset), (4 - offset, 7 - offset, 1 - offset), (7,), (1,)


def arrived_rows(offset):
    return (4 + offset,), (4 - offset,), (1, 1 + offset), (7, 7 + offset), (1 - offset,), (7 - offset,)


def sent_tiles(offset):
    return (7, 7 + offset), (1, 1 + offset), (4 - offset,), (7 - offset,), (1 - offset,), (4 + offset,)


def arrived_tiles(offset):
    return (1,), (7,), (4 - offset,), (1 - offset,), (7 - offset,), (4 + offset, 1 + offset, 7 + offset)


STAGES = ((0, 1), (2, 3), (4, 5))


def neighbour_of(cell):
    return cell - jnp.where(cell > 4, 1, 0)


def pack_kernel(send_hbm, p_hbm, *rest):
    outs, (send_ref, p_ref, sems) = rest[:-3], rest[-3:]
    ghosts = send_ref.shape[0]
    copies = [
        pltpu.make_async_copy(send_hbm, send_ref, sems.at[0]),
        pltpu.make_async_copy(p_hbm, p_ref, sems.at[1]),
    ]
    for copy in copies:
        copy.start()
    for copy in copies:
        copy.wait()
    for out, cells in zip(outs, sent_rows(pair_offset())):
        for at, cell in enumerate(cells):
            p = neighbour_of(cell)
            for g in range(ghosts):
                out[at * ghosts + g] = p_ref[send_ref[g, 0, p]]


def pack(send_rows, p_strips):
    ghosts = send_rows.shape[2]
    send = send_rows.transpose(2, 0, 1)
    return pl.pallas_call(
        pack_kernel,
        out_shape=[
            pltpu.VMEM((len(cells) * ghosts,) + p_strips.shape[1:], p_strips.dtype)
            for cells in sent_rows(1)
        ],
        in_specs=[HBM, HBM],
        out_specs=[VMEM] * 4,
        scratch_shapes=[
            pltpu.SMEM(send.shape, jnp.int32),
            pltpu.VMEM(p_strips.shape, p_strips.dtype),
            pltpu.SemaphoreType.DMA((2,)),
        ],
        compiler_params=PARAMS,
        name="pack",
    )(
        pltpu.with_memory_space_constraint(send, pltpu.HBM),
        pltpu.with_memory_space_constraint(p_strips, pltpu.HBM),
    )


def local_kernel(ghosts, slots, nbr_ref, ap_ref, a_ref, p_ref, *rest):
    even_ref, odd_ref, ga_ref, pt_ref, info_ref, order_ref, stage_ref, middle_ref = rest
    blocks, pieces, elements = ap_ref.shape
    kb = a_ref.shape[1]
    kc = p_ref.shape[2] // pieces
    stride = slots + 1
    stages = len(STAGES)
    capacity = ga_ref.shape[0]
    offset = pair_offset()
    for cell in (0, 1, 2, 3, 5, 6, 7, 8):
        stage = jnp.int32(cell // 3 != 1)
        if cell // 3 != 1 and cell % 3 != 1:
            stage = 1 + (cell % 3 - 1 == -offset).astype(jnp.int32)
        for g in range(ghosts):
            stage_ref[(cell - (cell > 4)) * ghosts + g] = stage

    def element(e, carry):
        counts, members = list(carry[:stages]), list(carry[stages:])
        for ref in (even_ref, odd_ref):
            ref[pl.ds(e * stride, stride)] = jnp.zeros((stride,) + ref.shape[1:], jnp.float32)
        last = jnp.int32(0)
        for j in range(blocks):
            n = nbr_ref[j, e]
            ghost = n >= elements
            a = a_ref[e, :, j * kb : (j + 1) * kb]
            product = jnp.dot(
                a, p_ref[jnp.where(ghost, 0, n)], preferred_element_type=jnp.float32
            )
            for k in range(pieces):
                row = e * stride + jnp.where(ghost, slots, ap_ref[j, k, e])
                piece = product[:, (k // 2) * 2 * kc : (k // 2 + 1) * 2 * kc]
                ref = odd_ref if k % 2 else even_ref
                ref[row] += piece
            if j > 0:
                stage = jnp.where(ghost, stage_ref[jnp.where(ghost, n - elements, 0)], 0)
                at = counts[0]
                for s in range(1, stages):
                    at = jnp.where(stage == s, s * capacity + counts[s], at)
                for k in range(pieces):
                    info_ref[at * (pieces + 2) + k] = e * stride + ap_ref[j, k, e]
                info_ref[at * (pieces + 2) + pieces] = n - elements
                listed = sum(counts)
                info_ref[at * (pieces + 2) + pieces + 1] = listed
                ga_ref[listed] = a
                for s in range(stages):
                    counts[s] += (ghost & (stage == s)).astype(jnp.int32)
                last = jnp.maximum(last, stage)
        first, middle, final = members
        order_ref[jnp.where(last == 2, elements - 1 - final, first)] = e
        middle_ref[middle] = e
        for s in range(stages):
            members[s] += (last == s).astype(jnp.int32)
        pt = p_ref[e].astype(jnp.float32).T.reshape(pieces, 2, kc // 2, kb)
        pt_ref[e, :, :kb] = pt[:, 0].reshape(pieces * kc // 2, kb).astype(jnp.bfloat16)
        pt_ref[e, :, kb:] = pt[:, 1].reshape(pieces * kc // 2, kb).astype(jnp.bfloat16)
        return *counts, *members

    totals = lax.fori_loop(0, elements, element, (jnp.int32(0),) * (2 * stages))
    counts, (first, middle, _) = totals[:stages], totals[stages:]

    def place(i, carry):
        order_ref[first + i] = middle_ref[i]
        return carry

    lax.fori_loop(0, middle, place, 0)
    for s in range(stages):
        for u in range(GROUP):
            at = s * capacity + counts[s] + u
            for k in range(pieces):
                info_ref[at * (pieces + 2) + k] = slots
            info_ref[at * (pieces + 2) + pieces] = 0
            info_ref[at * (pieces + 2) + pieces + 1] = 0
        order_ref[elements + s] = (counts[s] + GROUP - 1) // GROUP
    order_ref[elements + stages] = 0
    order_ref[elements + stages + 1] = first // STEP
    order_ref[elements + stages + 2] = (first + middle) // STEP
    order_ref[elements + stages + 3] = elements // STEP


def local_part(a_strips, p_strips, nbr_local, ap_slot, slots, ghosts):
    elements, kb, _ = a_strips.shape
    blocks, pieces = ap_slot.shape[1:]
    kc = p_strips.shape[2] // pieces
    capacity = elements * (blocks - 1) + GROUP
    sums = pltpu.VMEM((elements * (slots + 1), kb, 2 * kc), jnp.float32)
    return pl.pallas_call(
        functools.partial(local_kernel, ghosts, slots),
        out_shape=[
            sums,
            sums,
            pltpu.VMEM((capacity, kb, kb), jnp.bfloat16),
            pltpu.VMEM((elements, pieces * kc // 2, 2 * kb), jnp.bfloat16),
            pltpu.SMEM((len(STAGES) * capacity * (pieces + 2),), jnp.int32),
            pltpu.SMEM((elements + 2 * len(STAGES) + 1,), jnp.int32),
        ],
        in_specs=[SMEM, SMEM, VMEM, VMEM],
        out_specs=[VMEM] * 4 + [SMEM] * 2,
        scratch_shapes=[pltpu.SMEM((8 * ghosts,), jnp.int32), pltpu.SMEM((elements + 1,), jnp.int32)],
        compiler_params=PARAMS,
        cost_estimate=pl.CostEstimate(flops=5 * 10**9, bytes_accessed=10**7, transcendentals=0),
        name="local_part",
    )(scalar(nbr_local.T), scalar(ap_slot.transpose(1, 2, 0)), a_strips, p_strips)


def finish_kernel(stage, info_ref, order_ref, tile_ref, ga_ref, pt_ref, *rest):
    parts = STAGES[stage]
    stages = len(STAGES)
    arrived, rest = rest[: len(parts)], rest[len(parts) :]
    rest = rest[2 + SUMS * (stage > 0) :]
    even_ref, odd_ref, *tiles = rest[: 2 + SUMS]
    sent, ghost_ref = rest[2 + SUMS : -1], rest[-1]
    pieces, slots, elements = tile_ref.shape
    kb, kc2 = even_ref.shape[1:]
    half = kc2 // 4
    stride = slots + 1
    ghosts = ghost_ref.shape[0] // 8
    first = ga_ref.shape[0] * stage
    offset = pair_offset()
    for part, ref in zip(parts, arrived):
        for at, cell in enumerate(arrived_rows(offset)[part]):
            rows = pl.ds(neighbour_of(cell) * ghosts, ghosts)
            ghost_ref[rows] = ref[at * ghosts : (at + 1) * ghosts]
    if stage == 0:
        for ref in tiles:
            ref[...] = jnp.zeros_like(ref)
    left = lax.broadcasted_iota(jnp.int32, (kb, kc2), 1) < kc2 // 2

    def ghost_group(i, carry):
        for u in range(GROUP):
            at = first + i * GROUP + u
            product = jnp.dot(
                ga_ref[info_ref[at * (pieces + 2) + pieces + 1]],
                ghost_ref[info_ref[at * (pieces + 2) + pieces]],
                preferred_element_type=jnp.float32,
            )
            for k in range(pieces):
                ref = odd_ref if k % 2 else even_ref
                ref[info_ref[at * (pieces + 2) + k]] += product[
                    :, (k // 2) * kc2 : (k // 2 + 1) * kc2
                ]
        return carry

    lax.fori_loop(0, order_ref[elements + stage], ghost_group, 0)
    zero = jnp.zeros((kb, kc2), jnp.bfloat16)

    def one(e):
        pt = pt_ref[e]
        for pair in range(slots // 2):
            columns = []
            for q in (2 * pair, 2 * pair + 1):
                x = jnp.where(left, even_ref[e * stride + q], odd_ref[e * stride + q])
                y = (x + pltpu.roll(x, kc2 // 2, 1)).astype(jnp.bfloat16)
                columns.append(
                    jnp.concatenate([jnp.where(left, y, zero), jnp.where(left, zero, y)], axis=0)
                )
            terms = jnp.dot(
                pt, jnp.concatenate(columns, axis=1), preferred_element_type=jnp.float32
            )
            for k in range(pieces):
                for u in range(2):
                    ref = tiles[(2 * k + u) % SUMS]
                    ref[tile_ref[k, 2 * pair + u, e]] += terms[
                        k * half : (k + 1) * half, u * kc2 : (u + 1) * kc2
                    ]

    def step(i, carry, size=STEP):
        for u in range(size):
            one(order_ref[i + u])
        return carry

    begin, end = order_ref[elements + stages + stage], order_ref[elements + stages + stage + 1]
    doubles = (end - begin) // 3
    lax.fori_loop(0, doubles, lambda i, carry: step((begin + 3 * i) * STEP, carry, 3 * STEP), 0)

    lax.fori_loop(begin + 3 * doubles, end, lambda i, carry: step(i * STEP, carry), 0)

    if stage < stages - 1:
        return
    capacity = sent[-1].shape[0]

    def total(cell):
        rows = pl.ds(cell * capacity, capacity)
        return functools.reduce(jnp.add, [ref[rows] for ref in tiles])

    for out, cells in zip(sent, sent_tiles(offset)):
        for at, cell in enumerate(cells):
            out[at * capacity : (at + 1) * capacity] = total(cell).astype(out.dtype)
    sent[-1][...] = total(4)


def finish(stage, info, order, tile_slot, ga, pt, arrived, sums, tiles_total):
    parts = STAGES[stage]
    kb, kc2 = sums[0].shape[1:]
    half = kc2 // 4
    capacity = tiles_total // 9
    out_shape = [pltpu.VMEM(x.shape, x.dtype) for x in sums[:2]]
    out_shape += [pltpu.VMEM((tiles_total, half, kc2), jnp.float32)] * SUMS
    if stage == len(STAGES) - 1:
        out_shape += [
            pltpu.VMEM((len(cells) * capacity, half, kc2), jnp.bfloat16) for cells in sent_tiles(1)
        ]
        out_shape += [pltpu.VMEM((capacity, half, kc2), jnp.float32)]
    inputs = 5 + len(parts)
    return pl.pallas_call(
        functools.partial(finish_kernel, stage),
        out_shape=out_shape,
        in_specs=[SMEM] * 3 + [VMEM] * (2 + len(parts) + len(sums)),
        out_specs=[VMEM] * len(out_shape),
        scratch_shapes=[
            pltpu.VMEM((8 * arrived[4].shape[0],) + arrived[4].shape[1:], jnp.bfloat16)
        ],
        input_output_aliases={inputs + i: i for i in range(len(sums))},
        compiler_params=PARAMS,
        cost_estimate=pl.CostEstimate(flops=2 * 10**9, bytes_accessed=10**6, transcendentals=0),
        name=("first_part", "middle_part", "last_part")[stage],
    )(
        scalar(info),
        scalar(order),
        scalar(tile_slot.transpose(1, 2, 0)),
        resident(ga),
        resident(pt),
        *(resident(arrived[part]) for part in parts),
        *sums,
    )


def add_tiles(owner_ref, sums, cell, parcel, at, capacity):
    for g in range(capacity):
        ref = sums[g % len(sums)]
        ref[owner_ref[0, cell * capacity + g]] += parcel[at * capacity + g].astype(jnp.float32)


def first_sums_kernel(owner_ref, own, *rest):
    sums, small = rest[:-1], rest[-1]
    for ref in sums:
        ref[...] = jnp.zeros_like(ref)
    add_tiles(owner_ref, sums, 4, own, 0, own.shape[0])
    small[...] = jnp.zeros_like(small)


def first_sums(owner_map, own):
    _, half, kc2 = own.shape
    *sums, small = pl.pallas_call(
        first_sums_kernel,
        out_shape=[pltpu.VMEM((OWN, half, kc2), jnp.float32)] * OWNER_SUMS
        + [jax.ShapeDtypeStruct((8, 128), jnp.float32)],
        in_specs=[SMEM, VMEM],
        out_specs=[VMEM] * (OWNER_SUMS + 1),
        compiler_params=PARAMS,
        cost_estimate=pl.CostEstimate(flops=10**9, bytes_accessed=10**6, transcendentals=0),
        name="first_sums",
    )(scalar(owner_map), resident(own))
    return sums, small


def more_sums_kernel(owner_ref, *rest):
    arrived, sums = rest[: -2 * OWNER_SUMS], rest[-OWNER_SUMS:]
    capacity = owner_ref.shape[1] // 9
    for parcel, cells in zip(arrived, arrived_tiles(pair_offset())):
        add_tiles(owner_ref, sums, cells[0], parcel, 0, capacity)


def more_sums(owner_map, sums, arrived):
    inputs = 1 + len(arrived)
    return pl.pallas_call(
        more_sums_kernel,
        out_shape=[pltpu.VMEM(x.shape, x.dtype) for x in sums],
        in_specs=[SMEM] + [VMEM] * (len(arrived) + len(sums)),
        out_specs=[VMEM] * len(sums),
        input_output_aliases={inputs + i: i for i in range(len(sums))},
        compiler_params=PARAMS,
        cost_estimate=pl.CostEstimate(flops=2 * 10**10, bytes_accessed=10**6, transcendentals=0),
        name="more_sums",
    )(scalar(owner_map), *map(resident, arrived), *sums)


def owner_kernel(owner_ref, *rest):
    sums, (out_ref, stage_ref, sems) = rest[-3 - OWNER_SUMS : -3], rest[-3:]
    capacity = owner_ref.shape[1] // 9
    for parcel, cells in zip(rest, arrived_tiles(pair_offset())[3:]):
        for at, cell in enumerate(cells):
            add_tiles(owner_ref, sums, cell, parcel, at, capacity)
    owned, half, kc2 = sums[0].shape
    left = lax.broadcasted_iota(jnp.int32, (8, kc2), 1) < kc2 // 2
    copies = []
    for row in range(0, half, 8):
        for i in range(owned // 2):
            first = functools.reduce(jnp.add, [ref[2 * i, row : row + 8] for ref in sums])
            second = functools.reduce(jnp.add, [ref[2 * i + 1, row : row + 8] for ref in sums])
            columns = pl.ds(i * kc2, kc2)
            stage_ref[row : row + 8, columns] = jnp.where(
                left, first, pltpu.roll(second, kc2 // 2, 1)
            )
            stage_ref[half + row : half + row + 8, columns] = jnp.where(
                left, pltpu.roll(first, kc2 // 2, 1), second
            )
        for at in (row, half + row):
            rows = pl.ds(at, 8)
            copies.append(
                pltpu.make_async_copy(stage_ref.at[rows], out_ref.at[rows], sems.at[len(copies)])
            )
            copies[-1].start()
    for copy in copies:
        copy.wait()


def owner_sums(owner_map, sums, small, parcels):
    _, half, kc2 = sums[0].shape
    out = jax.ShapeDtypeStruct((2 * half, OWN * kc2 // 2), jnp.float32)
    results = pl.pallas_call(
        owner_kernel,
        out_shape=[pltpu.VMEM(x.shape, x.dtype) for x in sums] + [out],
        in_specs=[SMEM] + [VMEM] * (len(parcels) + len(sums)) + [HBM],
        out_specs=[VMEM] * len(sums) + [HBM],
        scratch_shapes=[
            pltpu.VMEM(out.shape, out.dtype),
            pltpu.SemaphoreType.DMA((2 * half // 8,)),
        ],
        input_output_aliases={1 + len(parcels) + i: i for i in range(len(sums))},
        compiler_params=PARAMS,
        name="owner_sums",
    )(scalar(owner_map), *map(resident, parcels), *sums, small)
    return results[-1]


def body(a_strips, p_strips, nbr_local, ap_slot, tile_slot, send_rows, owner_map):
    tiles_total = owner_map.shape[1]

    def local_work(nbr):
        return local_part(
            a_strips, p_strips, nbr, ap_slot, tile_slot.shape[2], send_rows.shape[2]
        )

    (*sums, ga, pt, info, order), arrived = exchange_rows(
        pack(send_rows, p_strips), nbr_local, local_work
    )
    for stage in range(len(STAGES)):
        sums = finish(stage, info, order, tile_slot, ga, pt, arrived, sums, tiles_total)
    *parcels, own = sums[2 + SUMS :]
    sums, small, parcels = exchange_tiles(parcels, functools.partial(first_sums, owner_map, own))
    sums = more_sums(owner_map, sums, parcels[:3])
    return owner_sums(owner_map, sums, small, parcels[3:])


def solution(mesh):
    placed = (
        P(("dom", "grp"), None, None),
        P(("dom", "grp"), None, None),
        P(("dom", "grp"), None),
        P(("dom", "grp"), None, None),
        P(("dom", "grp"), None, None),
        P(("dom", "grp"), None, None),
        P(("dom", "grp"), None),
    )
    return jax.shard_map(
        body, mesh=mesh, in_specs=placed, out_specs=P(None, ("dom", "grp")), check_vma=False
    )
```

```python
import functools

import jax
import jax.numpy as jnp
from jax import lax
from jax.experimental import pallas as pl
from jax.experimental.pallas import tpu as pltpu
from jax.sharding import PartitionSpec as P

OWN = 128
GROUP = 12
STEP = 4
SUMS = 4
OWNER_SUMS = 1
SMEM = pl.BlockSpec(memory_space=pltpu.SMEM)
VMEM = pl.BlockSpec(memory_space=pltpu.VMEM)
HBM = pl.BlockSpec(memory_space=pltpu.HBM)
PARAMS = pltpu.CompilerParams(vmem_limit_bytes=8 * 1024 * 1024)


def partner(index, kind, count):
    if kind == "pair":
        return index ^ 1
    if kind == "far":
        return (index - 1 + 2 * (index % 2)) % count
    return index


def moved(x, row, column):
    rows, columns = lax.axis_size("dom"), lax.axis_size("grp")
    pairs = [
        (i * columns + j, partner(i, row, rows) * columns + partner(j, column, columns))
        for i in range(rows)
        for j in range(columns)
    ]
    return lax.ppermute(x, ("dom", "grp"), pairs)


def resident(x):
    return pltpu.with_memory_space_constraint(x, pltpu.VMEM)


def scalar(x):
    return pltpu.with_memory_space_constraint(x, pltpu.SMEM)


def exchange_rows(parts, nbr_local, local_work):
    pair, far, near, away = parts
    size = near.shape[0]
    pair, far = moved(pair, "own", "pair"), moved(far, "own", "far")
    near = jnp.concatenate([near, pair[size : 2 * size]])
    away = jnp.concatenate([away, pair[2 * size :]])
    near, away, nbr_local = lax.optimization_barrier((near, away, nbr_local))
    *results, small = local_work(nbr_local)
    far, small = lax.optimization_barrier((far, small))
    near, away = moved(near, "pair", "own"), moved(away, "far", "own")
    near_far = moved(far[size : 2 * size], "pair", "own")
    away_far = moved(far[2 * size :], "far", "own")
    return (*results, small), (pair, far, near, away, near_far, away_far)


def exchange_tiles(parts, first_sums):
    near, away, far, near_far, away_far, pair = parts
    size = pair.shape[0]
    near, away = moved(near, "pair", "own"), moved(away, "far", "own")
    far = moved(far, "own", "far")
    sums, small = first_sums()
    near_far, away_far = moved(near_far, "pair", "far"), moved(away_far, "far", "far")
    near, away, small = lax.optimization_barrier((near, away, small))
    pair = moved(jnp.concatenate([pair, near[size:], away[size:]]), "own", "pair")
    return sums, small, (near, away, far, near_far, away_far, pair)


def offsets():
    return 3 - 6 * (lax.axis_index("dom") % 2), 1 - 2 * (lax.axis_index("grp") % 2)


def sent_rows(row, column):
    pair, far = 4 + column, 4 - column
    return (pair, pair + row, pair - row), (far, far + row, far - row), (4 + row,), (4 - row,)


def arrived_rows(row, column):
    pair, far = 4 + column, 4 - column
    return (pair,), (far,), (4 + row, pair + row), (4 - row, pair - row), (far + row,), (far - row,)


def sent_tiles(row, column):
    pair, far = 4 + column, 4 - column
    return (4 + row, pair + row), (4 - row, pair - row), (far,), (far + row,), (far - row,), (pair,)


def arrived_tiles(row, column):
    pair, far = 4 + column, 4 - column
    return (4 + row,), (4 - row,), (far,), (far + row,), (far - row,), (pair, pair + row, pair - row)


STAGES = ((0, 1), (2, 3), (4, 5))


def neighbour_of(cell):
    return cell - jnp.where(cell > 4, 1, 0)


def pack_kernel(send_hbm, p_hbm, *rest):
    outs, (send_ref, p_ref, sems) = rest[:-3], rest[-3:]
    ghosts = send_ref.shape[0]
    copies = [
        pltpu.make_async_copy(send_hbm, send_ref, sems.at[0]),
        pltpu.make_async_copy(p_hbm, p_ref, sems.at[1]),
    ]
    for copy in copies:
        copy.start()
    for copy in copies:
        copy.wait()
    for out, cells in zip(outs, sent_rows(*offsets())):
        for at, cell in enumerate(cells):
            p = neighbour_of(cell)
            for g in range(ghosts):
                out[at * ghosts + g] = p_ref[send_ref[g, 0, p]]


def pack(send_rows, p_strips):
    ghosts = send_rows.shape[2]
    send = send_rows.transpose(2, 0, 1)
    return pl.pallas_call(
        pack_kernel,
        out_shape=[
            pltpu.VMEM((len(cells) * ghosts,) + p_strips.shape[1:], p_strips.dtype)
            for cells in sent_rows(3, 1)
        ],
        in_specs=[HBM, HBM],
        out_specs=[VMEM] * 4,
        scratch_shapes=[
            pltpu.SMEM(send.shape, jnp.int32),
            pltpu.VMEM(p_strips.shape, p_strips.dtype),
            pltpu.SemaphoreType.DMA((2,)),
        ],
        compiler_params=PARAMS,
        name="pack",
    )(
        pltpu.with_memory_space_constraint(send, pltpu.HBM),
        pltpu.with_memory_space_constraint(p_strips, pltpu.HBM),
    )


def local_kernel(ghosts, slots, nbr_ref, ap_ref, a_ref, p_ref, *rest):
    even_ref, odd_ref, ga_ref, pt_ref, info_ref, order_ref, stage_ref, middle_ref = rest
    blocks, pieces, elements = ap_ref.shape
    kb = a_ref.shape[1]
    kc = p_ref.shape[2] // pieces
    stride = slots + 1
    stages = len(STAGES)
    capacity = ga_ref.shape[0]
    offset = offsets()[1]
    for cell in (0, 1, 2, 3, 5, 6, 7, 8):
        stage = jnp.int32(cell // 3 != 1)
        if cell // 3 != 1 and cell % 3 != 1:
            stage = 1 + (cell % 3 - 1 == -offset).astype(jnp.int32)
        for g in range(ghosts):
            stage_ref[(cell - (cell > 4)) * ghosts + g] = stage

    def element(e, carry):
        counts, members = list(carry[:stages]), list(carry[stages:])
        for ref in (even_ref, odd_ref):
            ref[pl.ds(e * stride, stride)] = jnp.zeros((stride,) + ref.shape[1:], jnp.float32)
        last = jnp.int32(0)
        for j in range(blocks):
            n = nbr_ref[j, e]
            ghost = n >= elements
            a = a_ref[e, :, j * kb : (j + 1) * kb]
            product = jnp.dot(
                a, p_ref[jnp.where(ghost, 0, n)], preferred_element_type=jnp.float32
            )
            for k in range(pieces):
                row = e * stride + jnp.where(ghost, slots, ap_ref[j, k, e])
                piece = product[:, (k // 2) * 2 * kc : (k // 2 + 1) * 2 * kc]
                ref = odd_ref if k % 2 else even_ref
                ref[row] += piece
            if j > 0:
                stage = jnp.where(ghost, stage_ref[jnp.where(ghost, n - elements, 0)], 0)
                at = counts[0]
                for s in range(1, stages):
                    at = jnp.where(stage == s, s * capacity + counts[s], at)
                for k in range(pieces):
                    info_ref[at * (pieces + 2) + k] = e * stride + ap_ref[j, k, e]
                info_ref[at * (pieces + 2) + pieces] = n - elements
                listed = sum(counts)
                info_ref[at * (pieces + 2) + pieces + 1] = listed
                ga_ref[listed] = a
                for s in range(stages):
                    counts[s] += (ghost & (stage == s)).astype(jnp.int32)
                last = jnp.maximum(last, stage)
        first, middle, final = members
        order_ref[jnp.where(last == 2, elements - 1 - final, first)] = e
        middle_ref[middle] = e
        for s in range(stages):
            members[s] += (last == s).astype(jnp.int32)
        pt = p_ref[e].astype(jnp.float32).T.reshape(pieces, 2, kc // 2, kb)
        pt_ref[e, :, :kb] = pt[:, 0].reshape(pieces * kc // 2, kb).astype(jnp.bfloat16)
        pt_ref[e, :, kb:] = pt[:, 1].reshape(pieces * kc // 2, kb).astype(jnp.bfloat16)
        return *counts, *members

    totals = lax.fori_loop(0, elements, element, (jnp.int32(0),) * (2 * stages))
    counts, (first, middle, _) = totals[:stages], totals[stages:]

    def place(i, carry):
        order_ref[first + i] = middle_ref[i]
        return carry

    lax.fori_loop(0, middle, place, 0)
    for s in range(stages):
        for u in range(GROUP):
            at = s * capacity + counts[s] + u
            for k in range(pieces):
                info_ref[at * (pieces + 2) + k] = slots
            info_ref[at * (pieces + 2) + pieces] = 0
            info_ref[at * (pieces + 2) + pieces + 1] = 0
        order_ref[elements + s] = (counts[s] + GROUP - 1) // GROUP
    order_ref[elements + stages] = 0
    order_ref[elements + stages + 1] = first // STEP
    order_ref[elements + stages + 2] = (first + middle) // STEP
    order_ref[elements + stages + 3] = elements // STEP


def local_part(a_strips, p_strips, nbr_local, ap_slot, slots, ghosts):
    elements, kb, _ = a_strips.shape
    blocks, pieces = ap_slot.shape[1:]
    kc = p_strips.shape[2] // pieces
    capacity = elements * (blocks - 1) + GROUP
    sums = pltpu.VMEM((elements * (slots + 1), kb, 2 * kc), jnp.float32)
    return pl.pallas_call(
        functools.partial(local_kernel, ghosts, slots),
        out_shape=[
            sums,
            sums,
            pltpu.VMEM((capacity, kb, kb), jnp.bfloat16),
            pltpu.VMEM((elements, pieces * kc // 2, 2 * kb), jnp.bfloat16),
            pltpu.SMEM((len(STAGES) * capacity * (pieces + 2),), jnp.int32),
            pltpu.SMEM((elements + 2 * len(STAGES) + 1,), jnp.int32),
        ],
        in_specs=[SMEM, SMEM, VMEM, VMEM],
        out_specs=[VMEM] * 4 + [SMEM] * 2,
        scratch_shapes=[pltpu.SMEM((8 * ghosts,), jnp.int32), pltpu.SMEM((elements + 1,), jnp.int32)],
        compiler_params=PARAMS,
        cost_estimate=pl.CostEstimate(flops=5 * 10**9, bytes_accessed=10**7, transcendentals=0),
        name="local_part",
    )(scalar(nbr_local.T), scalar(ap_slot.transpose(1, 2, 0)), a_strips, p_strips)


def finish_kernel(stage, info_ref, order_ref, tile_ref, ga_ref, pt_ref, *rest):
    parts = STAGES[stage]
    stages = len(STAGES)
    arrived, rest = rest[: len(parts)], rest[len(parts) :]
    rest = rest[2 + SUMS * (stage > 0) :]
    even_ref, odd_ref, *tiles = rest[: 2 + SUMS]
    sent, ghost_ref = rest[2 + SUMS : -1], rest[-1]
    pieces, slots, elements = tile_ref.shape
    kb, kc2 = even_ref.shape[1:]
    half = kc2 // 4
    stride = slots + 1
    ghosts = ghost_ref.shape[0] // 8
    first = ga_ref.shape[0] * stage
    for part, ref in zip(parts, arrived):
        for at, cell in enumerate(arrived_rows(*offsets())[part]):
            rows = pl.ds(neighbour_of(cell) * ghosts, ghosts)
            ghost_ref[rows] = ref[at * ghosts : (at + 1) * ghosts]
    if stage == 0:
        for ref in tiles:
            ref[...] = jnp.zeros_like(ref)
    left = lax.broadcasted_iota(jnp.int32, (kb, kc2), 1) < kc2 // 2

    def ghost_group(i, carry):
        for u in range(GROUP):
            at = first + i * GROUP + u
            product = jnp.dot(
                ga_ref[info_ref[at * (pieces + 2) + pieces + 1]],
                ghost_ref[info_ref[at * (pieces + 2) + pieces]],
                preferred_element_type=jnp.float32,
            )
            for k in range(pieces):
                ref = odd_ref if k % 2 else even_ref
                ref[info_ref[at * (pieces + 2) + k]] += product[
                    :, (k // 2) * kc2 : (k // 2 + 1) * kc2
                ]
        return carry

    lax.fori_loop(0, order_ref[elements + stage], ghost_group, 0)
    zero = jnp.zeros((kb, kc2), jnp.bfloat16)

    def one(e):
        pt = pt_ref[e]
        for pair in range(slots // 2):
            columns = []
            for q in (2 * pair, 2 * pair + 1):
                x = jnp.where(left, even_ref[e * stride + q], odd_ref[e * stride + q])
                y = (x + pltpu.roll(x, kc2 // 2, 1)).astype(jnp.bfloat16)
                columns.append(
                    jnp.concatenate([jnp.where(left, y, zero), jnp.where(left, zero, y)], axis=0)
                )
            terms = jnp.dot(
                pt, jnp.concatenate(columns, axis=1), preferred_element_type=jnp.float32
            )
            for k in range(pieces):
                for u in range(2):
                    ref = tiles[(2 * k + u) % SUMS]
                    ref[tile_ref[k, 2 * pair + u, e]] += terms[
                        k * half : (k + 1) * half, u * kc2 : (u + 1) * kc2
                    ]

    def step(i, carry, size=STEP):
        for u in range(size):
            one(order_ref[i + u])
        return carry

    begin, end = order_ref[elements + stages + stage], order_ref[elements + stages + stage + 1]
    doubles = (end - begin) // 3
    lax.fori_loop(0, doubles, lambda i, carry: step((begin + 3 * i) * STEP, carry, 3 * STEP), 0)

    lax.fori_loop(begin + 3 * doubles, end, lambda i, carry: step(i * STEP, carry), 0)

    if stage < stages - 1:
        return
    capacity = sent[-1].shape[0]

    def total(cell):
        rows = pl.ds(cell * capacity, capacity)
        return functools.reduce(jnp.add, [ref[rows] for ref in tiles])

    for out, cells in zip(sent, sent_tiles(*offsets())):
        for at, cell in enumerate(cells):
            out[at * capacity : (at + 1) * capacity] = total(cell).astype(out.dtype)
    sent[-1][...] = total(4)


def finish(stage, info, order, tile_slot, ga, pt, arrived, sums, tiles_total):
    parts = STAGES[stage]
    kb, kc2 = sums[0].shape[1:]
    half = kc2 // 4
    capacity = tiles_total // 9
    out_shape = [pltpu.VMEM(x.shape, x.dtype) for x in sums[:2]]
    out_shape += [pltpu.VMEM((tiles_total, half, kc2), jnp.float32)] * SUMS
    if stage == len(STAGES) - 1:
        out_shape += [
            pltpu.VMEM((len(cells) * capacity, half, kc2), jnp.bfloat16) for cells in sent_tiles(3, 1)
        ]
        out_shape += [pltpu.VMEM((capacity, half, kc2), jnp.float32)]
    inputs = 5 + len(parts)
    return pl.pallas_call(
        functools.partial(finish_kernel, stage),
        out_shape=out_shape,
        in_specs=[SMEM] * 3 + [VMEM] * (2 + len(parts) + len(sums)),
        out_specs=[VMEM] * len(out_shape),
        scratch_shapes=[
            pltpu.VMEM((8 * arrived[4].shape[0],) + arrived[4].shape[1:], jnp.bfloat16)
        ],
        input_output_aliases={inputs + i: i for i in range(len(sums))},
        compiler_params=PARAMS,
        cost_estimate=pl.CostEstimate(flops=2 * 10**9, bytes_accessed=10**6, transcendentals=0),
        name=("first_part", "middle_part", "last_part")[stage],
    )(
        scalar(info),
        scalar(order),
        scalar(tile_slot.transpose(1, 2, 0)),
        resident(ga),
        resident(pt),
        *(resident(arrived[part]) for part in parts),
        *sums,
    )


def add_tiles(owner_ref, sums, cell, parcel, at, capacity):
    for g in range(capacity):
        ref = sums[g % len(sums)]
        ref[owner_ref[0, cell * capacity + g]] += parcel[at * capacity + g].astype(jnp.float32)


def first_sums_kernel(owner_ref, own, *rest):
    sums, small = rest[:-1], rest[-1]
    for ref in sums:
        ref[...] = jnp.zeros_like(ref)
    add_tiles(owner_ref, sums, 4, own, 0, own.shape[0])
    small[...] = jnp.zeros_like(small)


def first_sums(owner_map, own):
    _, half, kc2 = own.shape
    *sums, small = pl.pallas_call(
        first_sums_kernel,
        out_shape=[pltpu.VMEM((OWN, half, kc2), jnp.float32)] * OWNER_SUMS
        + [jax.ShapeDtypeStruct((8, 128), jnp.float32)],
        in_specs=[SMEM, VMEM],
        out_specs=[VMEM] * (OWNER_SUMS + 1),
        compiler_params=PARAMS,
        cost_estimate=pl.CostEstimate(flops=10**9, bytes_accessed=10**6, transcendentals=0),
        name="first_sums",
    )(scalar(owner_map), resident(own))
    return sums, small


def more_sums_kernel(owner_ref, *rest):
    arrived, sums = rest[: -2 * OWNER_SUMS], rest[-OWNER_SUMS:]
    capacity = owner_ref.shape[1] // 9
    for parcel, cells in zip(arrived, arrived_tiles(*offsets())):
        add_tiles(owner_ref, sums, cells[0], parcel, 0, capacity)


def more_sums(owner_map, sums, arrived):
    inputs = 1 + len(arrived)
    return pl.pallas_call(
        more_sums_kernel,
        out_shape=[pltpu.VMEM(x.shape, x.dtype) for x in sums],
        in_specs=[SMEM] + [VMEM] * (len(arrived) + len(sums)),
        out_specs=[VMEM] * len(sums),
        input_output_aliases={inputs + i: i for i in range(len(sums))},
        compiler_params=PARAMS,
        cost_estimate=pl.CostEstimate(flops=2 * 10**10, bytes_accessed=10**6, transcendentals=0),
        name="more_sums",
    )(scalar(owner_map), *map(resident, arrived), *sums)


def owner_kernel(owner_ref, *rest):
    sums, (out_ref, stage_ref, sems) = rest[-3 - OWNER_SUMS : -3], rest[-3:]
    capacity = owner_ref.shape[1] // 9
    for parcel, cells in zip(rest, arrived_tiles(*offsets())[3:]):
        for at, cell in enumerate(cells):
            add_tiles(owner_ref, sums, cell, parcel, at, capacity)
    owned, half, kc2 = sums[0].shape
    left = lax.broadcasted_iota(jnp.int32, (8, kc2), 1) < kc2 // 2
    copies = []
    for row in range(0, half, 8):
        for i in range(owned // 2):
            first = functools.reduce(jnp.add, [ref[2 * i, row : row + 8] for ref in sums])
            second = functools.reduce(jnp.add, [ref[2 * i + 1, row : row + 8] for ref in sums])
            columns = pl.ds(i * kc2, kc2)
            stage_ref[row : row + 8, columns] = jnp.where(
                left, first, pltpu.roll(second, kc2 // 2, 1)
            )
            stage_ref[half + row : half + row + 8, columns] = jnp.where(
                left, pltpu.roll(first, kc2 // 2, 1), second
            )
        for at in (row, half + row):
            rows = pl.ds(at, 8)
            copies.append(
                pltpu.make_async_copy(stage_ref.at[rows], out_ref.at[rows], sems.at[len(copies)])
            )
            copies[-1].start()
    for copy in copies:
        copy.wait()


def owner_sums(owner_map, sums, small, parcels):
    _, half, kc2 = sums[0].shape
    out = jax.ShapeDtypeStruct((2 * half, OWN * kc2 // 2), jnp.float32)
    results = pl.pallas_call(
        owner_kernel,
        out_shape=[pltpu.VMEM(x.shape, x.dtype) for x in sums] + [out],
        in_specs=[SMEM] + [VMEM] * (len(parcels) + len(sums)) + [HBM],
        out_specs=[VMEM] * len(sums) + [HBM],
        scratch_shapes=[
            pltpu.VMEM(out.shape, out.dtype),
            pltpu.SemaphoreType.DMA((2 * half // 8,)),
        ],
        input_output_aliases={1 + len(parcels) + i: i for i in range(len(sums))},
        compiler_params=PARAMS,
        name="owner_sums",
    )(scalar(owner_map), *map(resident, parcels), *sums, small)
    return results[-1]


def body(a_strips, p_strips, nbr_local, ap_slot, tile_slot, send_rows, owner_map):
    tiles_total = owner_map.shape[1]

    def local_work(nbr):
        return local_part(
            a_strips, p_strips, nbr, ap_slot, tile_slot.shape[2], send_rows.shape[2]
        )

    (*sums, ga, pt, info, order), arrived = exchange_rows(
        pack(send_rows, p_strips), nbr_local, local_work
    )
    for stage in range(len(STAGES)):
        sums = finish(stage, info, order, tile_slot, ga, pt, arrived, sums, tiles_total)
    *parcels, own = sums[2 + SUMS :]
    sums, small, parcels = exchange_tiles(parcels, functools.partial(first_sums, owner_map, own))
    sums = more_sums(owner_map, sums, parcels[:3])
    return owner_sums(owner_map, sums, small, parcels[3:])


def solution(mesh):
    placed = (
        P(("dom", "grp"), None, None),
        P(("dom", "grp"), None, None),
        P(("dom", "grp"), None),
        P(("dom", "grp"), None, None),
        P(("dom", "grp"), None, None),
        P(("dom", "grp"), None, None),
        P(("dom", "grp"), None),
    )
    return jax.shard_map(
        body, mesh=mesh, in_specs=placed, out_specs=P(None, ("dom", "grp")), check_vma=False
    )
```

```python
import functools

import jax
import jax.numpy as jnp
from jax import lax
from jax.experimental import pallas as pl
from jax.experimental.pallas import tpu as pltpu
from jax.sharding import PartitionSpec as P

OWN = 128
GROUP = 12
STEP = 4
SUMS = 4
OWNER_SUMS = 1
SMEM = pl.BlockSpec(memory_space=pltpu.SMEM)
VMEM = pl.BlockSpec(memory_space=pltpu.VMEM)
HBM = pl.BlockSpec(memory_space=pltpu.HBM)
PARAMS = pltpu.CompilerParams(vmem_limit_bytes=8 * 1024 * 1024)


def partner(index, kind, count):
    if kind == "pair":
        return index ^ 1
    if kind == "far":
        return (index - 1 + 2 * (index % 2)) % count
    return index


def moved(x, row, column):
    rows, columns = lax.axis_size("dom"), lax.axis_size("grp")
    pairs = [
        (i * columns + j, partner(i, row, rows) * columns + partner(j, column, columns))
        for i in range(rows)
        for j in range(columns)
    ]
    return lax.ppermute(x, ("dom", "grp"), pairs)


def resident(x):
    return pltpu.with_memory_space_constraint(x, pltpu.VMEM)


def scalar(x):
    return pltpu.with_memory_space_constraint(x, pltpu.SMEM)


def exchange_rows(parts, nbr_local, local_work):
    pair, far, near, away = parts
    size = near.shape[0]
    pair, far = moved(pair, "own", "pair"), moved(far, "own", "far")
    near = jnp.concatenate([near, pair[size : 2 * size]])
    away = jnp.concatenate([away, pair[2 * size :]])
    near, away, nbr_local = lax.optimization_barrier((near, away, nbr_local))
    *results, small = local_work(nbr_local)
    far, small = lax.optimization_barrier((far, small))
    near, away = moved(near, "pair", "own"), moved(away, "far", "own")
    near_far = moved(far[size : 2 * size], "pair", "own")
    away_far = moved(far[2 * size :], "far", "own")
    return (*results, small), (pair, far, near, away, near_far, away_far)


def exchange_tiles(parts, first_sums):
    near, away, far, near_far, away_far, pair = parts
    size = pair.shape[0]
    near, away = moved(near, "pair", "own"), moved(away, "far", "own")
    far = moved(far, "own", "far")
    sums, small = first_sums()
    near_far, away_far = moved(near_far, "pair", "far"), moved(away_far, "far", "far")
    near, away, small = lax.optimization_barrier((near, away, small))
    pair = moved(jnp.concatenate([pair, near[size:], away[size:]]), "own", "pair")
    return sums, small, (near, away, far, near_far, away_far, pair)


def offsets():
    return 3 - 6 * (lax.axis_index("dom") % 2), 1 - 2 * (lax.axis_index("grp") % 2)


def sent_rows(row, column):
    pair, far = 4 + column, 4 - column
    return (pair, pair + row, pair - row), (far, far + row, far - row), (4 + row,), (4 - row,)


def arrived_rows(row, column):
    pair, far = 4 + column, 4 - column
    return (pair,), (far,), (4 + row, pair + row), (4 - row, pair - row), (far + row,), (far - row,)


def sent_tiles(row, column):
    pair, far = 4 + column, 4 - column
    return (4 + row, pair + row), (4 - row, pair - row), (far,), (far + row,), (far - row,), (pair,)


def arrived_tiles(row, column):
    pair, far = 4 + column, 4 - column
    return (4 + row,), (4 - row,), (far,), (far + row,), (far - row,), (pair, pair + row, pair - row)


STAGES = ((0, 1), (2, 3), (4, 5))


def neighbour_of(cell):
    return cell - jnp.where(cell > 4, 1, 0)


def pack_rows(send_ref, p_ref, outs, parts):
    ghosts = send_ref.shape[0]
    for out, cells in zip(outs, parts):
        for at, cell in enumerate(cells):
            p = neighbour_of(cell)
            for g in range(ghosts):
                out[at * ghosts + g] = p_ref[send_ref[g, 0, p]]


def pack_first_kernel(send_hbm, p_hbm, pair_ref, p_ref, send_ref, sems):
    copies = [
        pltpu.make_async_copy(send_hbm, send_ref, sems.at[0]),
        pltpu.make_async_copy(p_hbm, p_ref, sems.at[1]),
    ]
    for copy in copies:
        copy.start()
    for copy in copies:
        copy.wait()
    pack_rows(send_ref, p_ref, [pair_ref], sent_rows(*offsets())[:1])


def pack_rest_kernel(send_ref, p_ref, *outs):
    pack_rows(send_ref, p_ref, outs, sent_rows(*offsets())[1:])


def pack(send_rows, p_strips):
    ghosts = send_rows.shape[2]
    send = send_rows.transpose(2, 0, 1)
    shapes = [
        pltpu.VMEM((len(cells) * ghosts,) + p_strips.shape[1:], p_strips.dtype)
        for cells in sent_rows(3, 1)
    ]
    pair, p_here, send = pl.pallas_call(
        pack_first_kernel,
        out_shape=[shapes[0], pltpu.VMEM(p_strips.shape, p_strips.dtype), pltpu.SMEM(send.shape, jnp.int32)],
        in_specs=[HBM, HBM],
        out_specs=[VMEM, VMEM, SMEM],
        scratch_shapes=[pltpu.SemaphoreType.DMA((2,))],
        compiler_params=PARAMS,
        name="pack_first",
    )(
        pltpu.with_memory_space_constraint(send, pltpu.HBM),
        pltpu.with_memory_space_constraint(p_strips, pltpu.HBM),
    )
    rest = pl.pallas_call(
        pack_rest_kernel,
        out_shape=shapes[1:],
        in_specs=[SMEM, VMEM],
        out_specs=[VMEM] * (len(shapes) - 1),
        compiler_params=PARAMS,
        name="pack_rest",
    )(scalar(send), resident(p_here))
    return (pair, *rest), p_here


def local_kernel(ghosts, slots, nbr_ref, ap_ref, a_ref, p_ref, *rest):
    even_ref, odd_ref, ga_ref, pt_ref, info_ref, order_ref, stage_ref, middle_ref = rest
    blocks, pieces, elements = ap_ref.shape
    kb = a_ref.shape[1]
    kc = p_ref.shape[2] // pieces
    stride = slots + 1
    stages = len(STAGES)
    capacity = ga_ref.shape[0]
    offset = offsets()[1]
    for cell in (0, 1, 2, 3, 5, 6, 7, 8):
        stage = jnp.int32(cell // 3 != 1)
        if cell // 3 != 1 and cell % 3 != 1:
            stage = 1 + (cell % 3 - 1 == -offset).astype(jnp.int32)
        for g in range(ghosts):
            stage_ref[(cell - (cell > 4)) * ghosts + g] = stage

    def element(e, carry):
        counts, members = list(carry[:stages]), list(carry[stages:])
        for ref in (even_ref, odd_ref):
            ref[pl.ds(e * stride, stride)] = jnp.zeros((stride,) + ref.shape[1:], jnp.float32)
        last = jnp.int32(0)
        for j in range(blocks):
            n = nbr_ref[j, e]
            ghost = n >= elements
            a = a_ref[e, :, j * kb : (j + 1) * kb]
            product = jnp.dot(
                a, p_ref[jnp.where(ghost, 0, n)], preferred_element_type=jnp.float32
            )
            for k in range(pieces):
                row = e * stride + jnp.where(ghost, slots, ap_ref[j, k, e])
                piece = product[:, (k // 2) * 2 * kc : (k // 2 + 1) * 2 * kc]
                ref = odd_ref if k % 2 else even_ref
                ref[row] += piece
            if j > 0:
                stage = jnp.where(ghost, stage_ref[jnp.where(ghost, n - elements, 0)], 0)
                at = counts[0]
                for s in range(1, stages):
                    at = jnp.where(stage == s, s * capacity + counts[s], at)
                for k in range(pieces):
                    info_ref[at * (pieces + 2) + k] = e * stride + ap_ref[j, k, e]
                info_ref[at * (pieces + 2) + pieces] = n - elements
                listed = sum(counts)
                info_ref[at * (pieces + 2) + pieces + 1] = listed
                ga_ref[listed] = a
                for s in range(stages):
                    counts[s] += (ghost & (stage == s)).astype(jnp.int32)
                last = jnp.maximum(last, stage)
        first, middle, final = members
        order_ref[jnp.where(last == 2, elements - 1 - final, first)] = e
        middle_ref[middle] = e
        for s in range(stages):
            members[s] += (last == s).astype(jnp.int32)
        pt = p_ref[e].astype(jnp.float32).T.reshape(pieces, 2, kc // 2, kb)
        pt_ref[e, :, :kb] = pt[:, 0].reshape(pieces * kc // 2, kb).astype(jnp.bfloat16)
        pt_ref[e, :, kb:] = pt[:, 1].reshape(pieces * kc // 2, kb).astype(jnp.bfloat16)
        return *counts, *members

    totals = lax.fori_loop(0, elements, element, (jnp.int32(0),) * (2 * stages))
    counts, (first, middle, _) = totals[:stages], totals[stages:]

    def place(i, carry):
        order_ref[first + i] = middle_ref[i]
        return carry

    lax.fori_loop(0, middle, place, 0)
    for s in range(stages):
        for u in range(GROUP):
            at = s * capacity + counts[s] + u
            for k in range(pieces):
                info_ref[at * (pieces + 2) + k] = slots
            info_ref[at * (pieces + 2) + pieces] = 0
            info_ref[at * (pieces + 2) + pieces + 1] = 0
        order_ref[elements + s] = (counts[s] + GROUP - 1) // GROUP
    order_ref[elements + stages] = 0
    order_ref[elements + stages + 1] = first // STEP
    order_ref[elements + stages + 2] = (first + middle) // STEP
    order_ref[elements + stages + 3] = elements // STEP


def local_part(a_strips, p_strips, nbr_local, ap_slot, slots, ghosts):
    elements, kb, _ = a_strips.shape
    blocks, pieces = ap_slot.shape[1:]
    kc = p_strips.shape[2] // pieces
    capacity = elements * (blocks - 1) + GROUP
    sums = pltpu.VMEM((elements * (slots + 1), kb, 2 * kc), jnp.float32)
    return pl.pallas_call(
        functools.partial(local_kernel, ghosts, slots),
        out_shape=[
            sums,
            sums,
            pltpu.VMEM((capacity, kb, kb), jnp.bfloat16),
            pltpu.VMEM((elements, pieces * kc // 2, 2 * kb), jnp.bfloat16),
            pltpu.SMEM((len(STAGES) * capacity * (pieces + 2),), jnp.int32),
            pltpu.SMEM((elements + 2 * len(STAGES) + 1,), jnp.int32),
        ],
        in_specs=[SMEM, SMEM, VMEM, VMEM],
        out_specs=[VMEM] * 4 + [SMEM] * 2,
        scratch_shapes=[pltpu.SMEM((8 * ghosts,), jnp.int32), pltpu.SMEM((elements + 1,), jnp.int32)],
        compiler_params=PARAMS,
        cost_estimate=pl.CostEstimate(flops=5 * 10**9, bytes_accessed=10**7, transcendentals=0),
        name="local_part",
    )(scalar(nbr_local.T), scalar(ap_slot.transpose(1, 2, 0)), a_strips, resident(p_strips))


def finish_kernel(stage, info_ref, order_ref, tile_ref, ga_ref, pt_ref, *rest):
    parts = STAGES[stage]
    stages = len(STAGES)
    arrived, rest = rest[: len(parts)], rest[len(parts) :]
    rest = rest[2 + SUMS * (stage > 0) :]
    even_ref, odd_ref, *tiles = rest[: 2 + SUMS]
    sent, ghost_ref = rest[2 + SUMS : -1], rest[-1]
    pieces, slots, elements = tile_ref.shape
    kb, kc2 = even_ref.shape[1:]
    half = kc2 // 4
    stride = slots + 1
    ghosts = ghost_ref.shape[0] // 8
    first = ga_ref.shape[0] * stage
    for part, ref in zip(parts, arrived):
        for at, cell in enumerate(arrived_rows(*offsets())[part]):
            rows = pl.ds(neighbour_of(cell) * ghosts, ghosts)
            ghost_ref[rows] = ref[at * ghosts : (at + 1) * ghosts]
    if stage == 0:
        for ref in tiles:
            ref[...] = jnp.zeros_like(ref)
    left = lax.broadcasted_iota(jnp.int32, (kb, kc2), 1) < kc2 // 2

    def ghost_group(i, carry):
        for u in range(GROUP):
            at = first + i * GROUP + u
            product = jnp.dot(
                ga_ref[info_ref[at * (pieces + 2) + pieces + 1]],
                ghost_ref[info_ref[at * (pieces + 2) + pieces]],
                preferred_element_type=jnp.float32,
            )
            for k in range(pieces):
                ref = odd_ref if k % 2 else even_ref
                ref[info_ref[at * (pieces + 2) + k]] += product[
                    :, (k // 2) * kc2 : (k // 2 + 1) * kc2
                ]
        return carry

    lax.fori_loop(0, order_ref[elements + stage], ghost_group, 0)
    zero = jnp.zeros((kb, kc2), jnp.bfloat16)

    def one(e):
        pt = pt_ref[e]
        for pair in range(slots // 2):
            columns = []
            for q in (2 * pair, 2 * pair + 1):
                x = jnp.where(left, even_ref[e * stride + q], odd_ref[e * stride + q])
                y = (x + pltpu.roll(x, kc2 // 2, 1)).astype(jnp.bfloat16)
                columns.append(
                    jnp.concatenate([jnp.where(left, y, zero), jnp.where(left, zero, y)], axis=0)
                )
            terms = jnp.dot(
                pt, jnp.concatenate(columns, axis=1), preferred_element_type=jnp.float32
            )
            for k in range(pieces):
                for u in range(2):
                    ref = tiles[(2 * k + u) % SUMS]
                    ref[tile_ref[k, 2 * pair + u, e]] += terms[
                        k * half : (k + 1) * half, u * kc2 : (u + 1) * kc2
                    ]

    def step(i, carry, size=STEP):
        for u in range(size):
            one(order_ref[i + u])
        return carry

    begin, end = order_ref[elements + stages + stage], order_ref[elements + stages + stage + 1]
    doubles = (end - begin) // 3
    lax.fori_loop(0, doubles, lambda i, carry: step((begin + 3 * i) * STEP, carry, 3 * STEP), 0)

    lax.fori_loop(begin + 3 * doubles, end, lambda i, carry: step(i * STEP, carry), 0)

    if stage < stages - 1:
        return
    capacity = sent[-1].shape[0]

    def total(cell):
        rows = pl.ds(cell * capacity, capacity)
        return functools.reduce(jnp.add, [ref[rows] for ref in tiles])

    for out, cells in zip(sent, sent_tiles(*offsets())):
        for at, cell in enumerate(cells):
            out[at * capacity : (at + 1) * capacity] = total(cell).astype(out.dtype)
    sent[-1][...] = total(4)


def finish(stage, info, order, tile_slot, ga, pt, arrived, sums, tiles_total):
    parts = STAGES[stage]
    kb, kc2 = sums[0].shape[1:]
    half = kc2 // 4
    capacity = tiles_total // 9
    out_shape = [pltpu.VMEM(x.shape, x.dtype) for x in sums[:2]]
    out_shape += [pltpu.VMEM((tiles_total, half, kc2), jnp.float32)] * SUMS
    if stage == len(STAGES) - 1:
        out_shape += [
            pltpu.VMEM((len(cells) * capacity, half, kc2), jnp.bfloat16) for cells in sent_tiles(3, 1)
        ]
        out_shape += [pltpu.VMEM((capacity, half, kc2), jnp.float32)]
    inputs = 5 + len(parts)
    return pl.pallas_call(
        functools.partial(finish_kernel, stage),
        out_shape=out_shape,
        in_specs=[SMEM] * 3 + [VMEM] * (2 + len(parts) + len(sums)),
        out_specs=[VMEM] * len(out_shape),
        scratch_shapes=[
            pltpu.VMEM((8 * arrived[4].shape[0],) + arrived[4].shape[1:], jnp.bfloat16)
        ],
        input_output_aliases={inputs + i: i for i in range(len(sums))},
        compiler_params=PARAMS,
        cost_estimate=pl.CostEstimate(flops=2 * 10**9, bytes_accessed=10**6, transcendentals=0),
        name=("first_part", "middle_part", "last_part")[stage],
    )(
        scalar(info),
        scalar(order),
        scalar(tile_slot.transpose(1, 2, 0)),
        resident(ga),
        resident(pt),
        *(resident(arrived[part]) for part in parts),
        *sums,
    )


def add_tiles(owner_ref, sums, cell, parcel, at, capacity):
    for g in range(capacity):
        ref = sums[g % len(sums)]
        ref[owner_ref[0, cell * capacity + g]] += parcel[at * capacity + g].astype(jnp.float32)


def first_sums_kernel(owner_ref, own, *rest):
    sums, small = rest[:-1], rest[-1]
    for ref in sums:
        ref[...] = jnp.zeros_like(ref)
    add_tiles(owner_ref, sums, 4, own, 0, own.shape[0])
    small[...] = jnp.zeros_like(small)


def first_sums(owner_map, own):
    _, half, kc2 = own.shape
    *sums, small = pl.pallas_call(
        first_sums_kernel,
        out_shape=[pltpu.VMEM((OWN, half, kc2), jnp.float32)] * OWNER_SUMS
        + [jax.ShapeDtypeStruct((8, 128), jnp.float32)],
        in_specs=[SMEM, VMEM],
        out_specs=[VMEM] * (OWNER_SUMS + 1),
        compiler_params=PARAMS,
        cost_estimate=pl.CostEstimate(flops=10**9, bytes_accessed=10**6, transcendentals=0),
        name="first_sums",
    )(scalar(owner_map), resident(own))
    return sums, small


def more_sums_kernel(owner_ref, *rest):
    arrived, sums = rest[: -2 * OWNER_SUMS], rest[-OWNER_SUMS:]
    capacity = owner_ref.shape[1] // 9
    for parcel, cells in zip(arrived, arrived_tiles(*offsets())):
        add_tiles(owner_ref, sums, cells[0], parcel, 0, capacity)


def more_sums(owner_map, sums, arrived):
    inputs = 1 + len(arrived)
    return pl.pallas_call(
        more_sums_kernel,
        out_shape=[pltpu.VMEM(x.shape, x.dtype) for x in sums],
        in_specs=[SMEM] + [VMEM] * (len(arrived) + len(sums)),
        out_specs=[VMEM] * len(sums),
        input_output_aliases={inputs + i: i for i in range(len(sums))},
        compiler_params=PARAMS,
        cost_estimate=pl.CostEstimate(flops=2 * 10**10, bytes_accessed=10**6, transcendentals=0),
        name="more_sums",
    )(scalar(owner_map), *map(resident, arrived), *sums)


def owner_kernel(owner_ref, *rest):
    sums, (out_ref, stage_ref, sems) = rest[-3 - OWNER_SUMS : -3], rest[-3:]
    capacity = owner_ref.shape[1] // 9
    for parcel, cells in zip(rest, arrived_tiles(*offsets())[2:]):
        for at, cell in enumerate(cells):
            add_tiles(owner_ref, sums, cell, parcel, at, capacity)
    owned, half, kc2 = sums[0].shape
    left = lax.broadcasted_iota(jnp.int32, (8, kc2), 1) < kc2 // 2
    copies = []
    for row in range(0, half, 8):
        for i in range(owned // 2):
            first = functools.reduce(jnp.add, [ref[2 * i, row : row + 8] for ref in sums])
            second = functools.reduce(jnp.add, [ref[2 * i + 1, row : row + 8] for ref in sums])
            columns = pl.ds(i * kc2, kc2)
            stage_ref[row : row + 8, columns] = jnp.where(
                left, first, pltpu.roll(second, kc2 // 2, 1)
            )
            stage_ref[half + row : half + row + 8, columns] = jnp.where(
                left, pltpu.roll(first, kc2 // 2, 1), second
            )
        for at in (row, half + row):
            rows = pl.ds(at, 8)
            copies.append(
                pltpu.make_async_copy(stage_ref.at[rows], out_ref.at[rows], sems.at[len(copies)])
            )
            copies[-1].start()
    for copy in copies:
        copy.wait()


def owner_sums(owner_map, sums, small, parcels):
    _, half, kc2 = sums[0].shape
    out = jax.ShapeDtypeStruct((2 * half, OWN * kc2 // 2), jnp.float32)
    results = pl.pallas_call(
        owner_kernel,
        out_shape=[pltpu.VMEM(x.shape, x.dtype) for x in sums] + [out],
        in_specs=[SMEM] + [VMEM] * (len(parcels) + len(sums)) + [HBM],
        out_specs=[VMEM] * len(sums) + [HBM],
        scratch_shapes=[
            pltpu.VMEM(out.shape, out.dtype),
            pltpu.SemaphoreType.DMA((2 * half // 8,)),
        ],
        input_output_aliases={1 + len(parcels) + i: i for i in range(len(sums))},
        compiler_params=PARAMS,
        name="owner_sums",
    )(scalar(owner_map), *map(resident, parcels), *sums, small)
    return results[-1]


def body(a_strips, p_strips, nbr_local, ap_slot, tile_slot, send_rows, owner_map):
    tiles_total = owner_map.shape[1]

    outgoing, p_here = pack(send_rows, p_strips)

    def local_work(nbr):
        return local_part(a_strips, p_here, nbr, ap_slot, tile_slot.shape[2], send_rows.shape[2])

    (*sums, ga, pt, info, order), arrived = exchange_rows(outgoing, nbr_local, local_work)
    for stage in range(len(STAGES)):
        sums = finish(stage, info, order, tile_slot, ga, pt, arrived, sums, tiles_total)
    *parcels, own = sums[2 + SUMS :]
    sums, small, parcels = exchange_tiles(parcels, functools.partial(first_sums, owner_map, own))
    sums = more_sums(owner_map, sums, parcels[:2])
    return owner_sums(owner_map, sums, small, parcels[2:])


def solution(mesh):
    placed = (
        P(("dom", "grp"), None, None),
        P(("dom", "grp"), None, None),
        P(("dom", "grp"), None),
        P(("dom", "grp"), None, None),
        P(("dom", "grp"), None, None),
        P(("dom", "grp"), None, None),
        P(("dom", "grp"), None),
    )
    return jax.shard_map(
        body, mesh=mesh, in_specs=placed, out_specs=P(None, ("dom", "grp")), check_vma=False
    )
```
